512 devices in a mesh: ctx: 64 (over z_hi, y, core), head: 8 (over x, z_lo).
Axes of the slice: x: 4, y: 8, z: 8 (z_hi: 4, z_lo: 2; z = z_hi * 2 + z_lo), core: 2. Of those that a mesh axis runs over, the one named last changes fastest.
Arguments:
- queries: bfloat16 [16384, 2048], P('ctx', 'head'), may hold values from -16.25 to 16.25
- keys: bfloat16 [16384, 256], P('ctx'), may hold values from -6 to 6
- values: bfloat16 [16384, 256], P('ctx'), may hold values from -48 to 48
Outputs:
- attn_out: bfloat16 [16384, 2048], P('ctx', 'head')
- hessian: float32 [2048, 2048], P('ctx', 'head')
The draws below stay inside these ranges and needn't reach their ends.
All inputs are finite; a program needn't handle non-finite values.
Results may differ from the reference program's by a relative error of at most 0.006.
Values may be sent and summed in bfloat16 or wider, within the bound.
No kernel may reach another device: no remote copies, remote signals or barrier semaphores. Data moves between devices by JAX's collectives and lax.ppermute only.
A program may use at most 128 MiB of HBM per device.

```python
import math
import jax
import jax.numpy as jnp
from jax import lax

HEADS = 16
KVG = 2
HD = 128
TOKENS = 16384


def draw_queries(key, part):
    key = jax.random.fold_in(key, 11)
    base = jnp.clip(1.5 * jax.random.normal(key, (TOKENS, HEADS * HD), jnp.float32), -6.0, 6.0)
    return base.astype(jnp.bfloat16)


def draw_keys(key, part):
    key = jax.random.fold_in(key, 12)
    base = jnp.clip(1.5 * jax.random.normal(key, (TOKENS, KVG * HD), jnp.float32), -6.0, 6.0)
    return base.astype(jnp.bfloat16)


def shard_levels(stream_key, extent, shards, smallest, high):
    loudness = 1.0
    for axis_at, blocks in shards:
        steps = jax.random.uniform(jax.random.fold_in(jax.random.fold_in(stream_key, 6), axis_at), (blocks,), jnp.float32, smallest / len(shards), high / len(shards))
        loudness = loudness * jnp.repeat(jnp.exp(steps), extent[axis_at] // blocks).reshape((-1,) + (1,) * (len(extent) - 1 - axis_at))
    return loudness


def noise(key, shape, width, reach, shards=(), kind=jnp.bfloat16):
    values = width * jax.random.normal(key, shape, jnp.float32)
    if shards:
        values = values * shard_levels(key, shape, shards, -0.22, 0.18)
    return jnp.clip(values, -reach, reach).astype(kind)


def setup_inputs(seed: int = 0) -> dict:
    key_of = jax.random.split(jax.random.key(seed), 4)
    return {
        "queries": draw_queries(jax.random.fold_in(key_of[3], 71), 0),
        "keys": draw_keys(jax.random.fold_in(key_of[3], 71), 0),
        "values": noise(key_of[2], (TOKENS, KVG * HD), 8.0, 48.0, ((0, 64),)),
    }


def reference(queries, keys, values):
    block = math.gcd(TOKENS, 256)
    per_group = HEADS // KVG
    key_grid = keys.astype(jnp.float32).reshape(TOKENS, KVG, HD)
    val_grid = values.astype(jnp.float32).reshape(TOKENS, KVG, HD)
    pieces = []
    for start in range(0, TOKENS, block):
        stop = start + block
        q_grid = queries[start:stop].astype(jnp.float32).reshape(block, KVG, per_group, HD)
        scores = jnp.einsum('bgjd,lgd->gjbl', q_grid, key_grid[:stop]) / math.sqrt(HD)
        rows = start + jnp.arange(block, dtype=jnp.int32)
        cols = jnp.arange(stop, dtype=jnp.int32)
        scores = jnp.where(cols[None, :] <= rows[:, None], scores, -jnp.inf)
        top = lax.optimization_barrier(jnp.max(scores, axis=-1, keepdims=True))
        weights = jnp.exp(scores - top)
        total = lax.optimization_barrier(jnp.sum(weights, axis=-1))
        coarse = lax.optimization_barrier(weights.astype(jnp.bfloat16)).astype(jnp.float32)
        mixed = jnp.einsum('gjbl,lgd->bgjd', coarse, val_grid[:stop])
        mixed = mixed / jnp.transpose(total, (2, 0, 1))[..., None]
        pieces.append(mixed.reshape(block, HEADS * HD).astype(jnp.bfloat16))
    attn_out = jnp.concatenate(pieces, axis=0)
    hessian = jnp.dot(attn_out.T, attn_out, preferred_element_type=jnp.float32) * (2.0 / TOKENS)
    return (attn_out, hessian)
```

```python
import math

import jax
import jax.numpy as jnp
from jax import lax
from jax.experimental import pallas as pl
from jax.experimental.pallas import tpu as pltpu
from jax.sharding import Mesh
from jax.sharding import PartitionSpec as P

HEADS = 16
KVG = 2
HD = 128
TOKENS = 16384

CTX = ("zh", "y", "c")
HEAD = ("g", "xl", "zl")
CHIPS = ("zh", "y")
SHARE = ("xl", "zl")
NZ, NY, NC, NS = 4, 8, 2, 4
TOK = 256
CUT = TOK // NS
TILE = NY * CUT
KEYS = NZ * TILE
SCALE = math.log2(math.e) / math.sqrt(HD)
LOW = -1e30
FLOOR = -1e29
STAT = 16


def dot_nt(a, b):
    return lax.dot_general(a, b, (((1,), (1,)), ((), ())), preferred_element_type=jnp.float32)


def dot_nn(a, b):
    return lax.dot_general(a, b, (((1,), (0,)), ((), ())), preferred_element_type=jnp.float32)


def attend_kernel(pos_ref, q_ref, own_ref, oth_ref, o_ref, s_ref, mx_ref, ve_ref, acc_ref):
    zh, y, c, u = pos_ref[0], pos_ref[1], pos_ref[2], pos_ref[3]
    ones = jnp.ones((KEYS, HD), jnp.bfloat16)
    for a, kv_ref in enumerate((own_ref, oth_ref)):
        ve_ref[a, :, 0:HD] = kv_ref[:, HD : 2 * HD]
        ve_ref[a, :, HD : 2 * HD] = ones
    lane = lax.broadcasted_iota(jnp.int32, (TOK, HD), 1)

    def one_part(up, _):
        stats = jnp.zeros((TOK, HD), jnp.float32)
        for hh in range(2):
            cols = slice(hh * HD, (hh + 1) * HD)
            q = q_ref[up, :, cols]
            mx_ref[...] = jnp.full((TOK, HD), LOW, jnp.float32)
            acc_ref[...] = jnp.zeros((TOK, 2 * HD), jnp.float32)

            def scores(zt, masked):
                for a, kv_ref in enumerate((own_ref, oth_ref)):
                    s = dot_nt(q, kv_ref[zt * TILE : (zt + 1) * TILE, 0:HD])
                    if masked:
                        n = lax.broadcasted_iota(jnp.int32, (TOK, TILE), 1)
                        r = lax.broadcasted_iota(jnp.int32, (TOK, TILE), 0)
                        side = c if a == 0 else 1 - c
                        k_pos = (n // CUT) * (2 * TOK) + n % CUT + side * TOK + u * CUT
                        s = jnp.where(k_pos <= r + (y * 2 + c) * TOK, s, LOW)
                    at = (2 * zt + a) * TILE
                    s_ref[:, at : at + TILE] = s
                    m = mx_ref[...]
                    for i in range(TILE // HD):
                        m = jnp.maximum(m, s[:, i * HD : (i + 1) * HD])
                    mx_ref[...] = m

            for zt in range(NZ):
                pl.when(zt < zh)(lambda zt=zt: scores(zt, False))
                pl.when(zt == zh)(lambda zt=zt: scores(zt, True))
            top = jnp.maximum(jnp.max(mx_ref[...], axis=1, keepdims=True), FLOOR) * SCALE

            def mix(zt):
                acc = acc_ref[...]
                for a in range(2):
                    at = (2 * zt + a) * TILE
                    w = jnp.exp2(s_ref[:, at : at + TILE] * SCALE - top).astype(jnp.bfloat16)
                    acc = acc + dot_nn(w, ve_ref[a, zt * TILE : (zt + 1) * TILE, :])
                acc_ref[...] = acc

            for zt in range(NZ):
                pl.when(zt <= zh)(lambda zt=zt: mix(zt))
            total = acc_ref[:, HD : 2 * HD]
            some = total > 0.0
            safe = jnp.where(some, total, 1.0)
            o_ref[up, 0:TOK, cols] = (acc_ref[:, 0:HD] / safe).astype(jnp.bfloat16)
            lse = jnp.where(some, top + jnp.log2(safe), LOW)
            hi = lse.astype(jnp.bfloat16).astype(jnp.float32)
            mid = (lse - hi).astype(jnp.bfloat16).astype(jnp.float32)
            low = lse - hi - mid
            for i, part in enumerate((hi, mid, low)):
                stats = jnp.where(lane == hh * 3 + i, part, stats)
        o_ref[up, TOK : TOK + STAT, :] = jnp.transpose(stats)[0:STAT].astype(jnp.bfloat16)
        return 0

    lax.fori_loop(0, NS, one_part, 0)


def combine_kernel(r_ref, x_ref):
    rows = [r_ref[s, TOK : TOK + STAT, :].astype(jnp.float32) for s in range(NS)]
    rows.append(jnp.zeros((HD - NS * STAT, TOK), jnp.float32))
    stats = jnp.transpose(jnp.concatenate(rows, axis=0))
    for hh in range(2):
        cols = slice(hh * HD, (hh + 1) * HD)
        lses = []
        for s in range(NS):
            at = s * STAT + hh * 3
            lses.append(stats[:, at : at + 1] + stats[:, at + 1 : at + 2] + stats[:, at + 2 : at + 3])
        top = jnp.maximum(jnp.maximum(lses[0], lses[1]), jnp.maximum(lses[2], lses[3]))
        w = [jnp.exp2(lse - top) for lse in lses]
        inv = 1.0 / (w[0] + w[1] + w[2] + w[3])
        x = jnp.zeros((TOK, HD), jnp.float32)
        for s in range(NS):
            x = x + r_ref[s, 0:TOK, cols].astype(jnp.float32) * (w[s] * inv)
        x_ref[:, cols] = x.astype(jnp.bfloat16)


def gram_kernel(r_ref, x_ref, h_ref):
    x = x_ref[...]
    for i in range(8):
        part = lax.dot_general(
            r_ref[i], x, (((0,), (0,)), ((), ())), preferred_element_type=jnp.float32
        )
        h_ref[i * 4 : (i + 1) * 4] = part.astype(jnp.bfloat16).reshape(4, 32, 2 * HD)


def vmem(n):
    return [pl.BlockSpec(memory_space=pltpu.VMEM)] * n


def local(queries, keys, values):
    zh, y, c = (lax.axis_index(a) for a in CTX)
    g = lax.axis_index("g")
    u = lax.axis_index(SHARE)
    swap = [(0, 1), (1, 0)]
    own = jnp.concatenate(
        [lax.dynamic_slice(part, (u * CUT, g * HD), (CUT, HD)) for part in (keys, values)], axis=1
    )
    with jax.named_scope("kv_gather"):
        kv_own = lax.all_to_all(
            jnp.broadcast_to(own[None], (NZ * NY, CUT, 2 * HD)), CHIPS, 0, 0
        ).reshape(KEYS, 2 * HD)
    with jax.named_scope("q_gather"):
        q_all = lax.all_to_all(jnp.broadcast_to(queries[None], (NS, TOK, 2 * HD)), SHARE, 0, 0)
    with jax.named_scope("kv_swap"):
        kv_oth = lax.ppermute(kv_own, "c", swap)
    pos = jnp.stack([zh, y, c, u]).astype(jnp.int32)
    part = pl.pallas_call(
        attend_kernel,
        out_shape=jax.ShapeDtypeStruct((NS, TOK + STAT, 2 * HD), jnp.bfloat16),
        in_specs=[pl.BlockSpec(memory_space=pltpu.SMEM)] + vmem(3),
        out_specs=vmem(1)[0],
        scratch_shapes=[
            pltpu.VMEM((TOK, 2 * KEYS), jnp.float32),
            pltpu.VMEM((TOK, HD), jnp.float32),
            pltpu.VMEM((2, KEYS, 2 * HD), jnp.bfloat16),
            pltpu.VMEM((TOK, 2 * HD), jnp.float32),
        ],
        compiler_params=pltpu.CompilerParams(vmem_limit_bytes=32 << 20),
        name="attend",
    )(pos, q_all, kv_own, kv_oth)
    with jax.named_scope("part_exchange"):
        parts = lax.all_to_all(part, SHARE, 0, 0)
    attn_out = pl.pallas_call(
        combine_kernel,
        out_shape=jax.ShapeDtypeStruct((TOK, 2 * HD), jnp.bfloat16),
        in_specs=vmem(1),
        out_specs=vmem(1)[0],
        compiler_params=pltpu.CompilerParams(vmem_limit_bytes=32 << 20),
        name="combine",
    )(parts)
    with jax.named_scope("x_swap"):
        attn_oth = lax.ppermute(attn_out, "c", swap)
    x = jnp.concatenate([attn_out, attn_oth], axis=0)
    col = jnp.arange(HD, dtype=jnp.int32)
    picked = (col // 32) * 64 + c * 32 + col % 32
    pick = (jnp.arange(2 * HD, dtype=jnp.int32)[:, None] == picked[None, :]).astype(jnp.bfloat16)
    x_half = jnp.dot(x, pick, preferred_element_type=jnp.float32).astype(jnp.bfloat16)
    with jax.named_scope("x_gather"):
        x_all = lax.all_to_all(jnp.broadcast_to(x_half[None], (8, 2 * TOK, HD)), HEAD, 0, 0)
    gram = pl.pallas_call(
        gram_kernel,
        out_shape=jax.ShapeDtypeStruct((NZ * NY, 32, 2 * HD), jnp.bfloat16),
        in_specs=vmem(2),
        out_specs=vmem(1)[0],
        compiler_params=pltpu.CompilerParams(vmem_limit_bytes=32 << 20),
        name="gram",
    )(x_all, x)
    with jax.named_scope("h_exchange"):
        h_parts = lax.all_to_all(gram, CHIPS, 0, 0)
    hessian = jnp.sum(h_parts.astype(jnp.float32), axis=0) * (2.0 / TOKENS)
    return attn_out, hessian


def solution(mesh):
    cut = Mesh(mesh.devices.reshape(NZ, NY, NC, 2, 2, 2), CTX + HEAD)
    in_specs = (P(CTX, HEAD), P(CTX, None), P(CTX, None))
    out_specs = (P(CTX, HEAD), P(CTX, HEAD))
    return jax.shard_map(local, mesh=cut, in_specs=in_specs, out_specs=out_specs, check_vma=False)
```

```python
import math

import jax
import jax.numpy as jnp
from jax import lax
from jax.experimental import pallas as pl
from jax.experimental.pallas import tpu as pltpu
from jax.sharding import Mesh
from jax.sharding import PartitionSpec as P

HEADS = 16
KVG = 2
HD = 128
TOKENS = 16384

CTX = ("zh", "y", "c")
HEAD = ("g", "xl", "zl")
CHIPS = ("zh", "y")
SHARE = ("xl", "zl")
NZ, NY, NC, NS = 4, 8, 2, 4
TOK = 256
CUT = TOK // NS
TILE = NY * CUT
WIDE = NC * TILE
KEYS = NZ * TILE
ROWS = NS * TOK
PIECE = 256
SCALE = math.log2(math.e) / math.sqrt(HD)
LOW = -1e30
FLOOR = -1e29
STAT = 16
ABC = (((1,), (0,)), ((), ()))
ATB = (((0,), (0,)), ((), ()))


def dot(a, b, dims=ABC):
    return lax.dot_general(a, b, dims, preferred_element_type=jnp.float32)


def iota(shape, dim):
    return lax.broadcasted_iota(jnp.int32, shape, dim)


def column(side, at):
    return (at // 32) * 64 + side * 32 + at % 32


def prep_kernel(pos_ref, k_ref, v_ref, o_ref):
    u, g = pos_ref[3], pos_ref[4]
    rows = pl.ds(pl.multiple_of(u * CUT, CUT), CUT)
    k = jnp.where(g == 0, k_ref[rows, 0:HD], k_ref[rows, HD : 2 * HD])
    v = jnp.where(g == 0, v_ref[rows, 0:HD], v_ref[rows, HD : 2 * HD])
    to = iota((HD, HD), 1)
    order = iota((HD, HD), 0) == column(to // 64, to % 64)
    v = dot(v, order.astype(jnp.bfloat16)).astype(jnp.bfloat16)
    for i in range(NZ * NY):
        o_ref[i, :, 0:HD] = k
        o_ref[i, :, HD : 2 * HD] = v


def attend_kernel(
    pos_ref, q0_ref, q1_ref, q2_ref, own_ref, oth_ref, o_ref, q_s, k_s, ve_s, s_s, mx_s, acc_s, st_s, o0_s
):
    zh, y, c, u = pos_ref[0], pos_ref[1], pos_ref[2], pos_ref[3]
    for zt in range(NZ):
        for a, kv_ref in enumerate((own_ref, oth_ref)):
            src = slice(zt * TILE, (zt + 1) * TILE)
            dst = slice(a * TILE, (a + 1) * TILE)
            k_s[zt, :, dst] = jnp.transpose(kv_ref[src, 0:HD])
            ve_s[zt, dst, 0:HD] = kv_ref[src, HD : 2 * HD]
            ve_s[zt, dst, HD : 2 * HD] = jnp.ones((TILE, HD), jnp.bfloat16)
    for hh in range(2):
        cols = slice(hh * HD, (hh + 1) * HD)
        for i, q in enumerate((q0_ref[:, cols], q1_ref[:, cols], q2_ref[0, :, cols], q2_ref[1, :, cols])):
            q_s[hh, i * TOK : (i + 1) * TOK, :] = q

    def body(zt, masked, new, old, top):
        if new is not None:
            q = q_s[new]
            m = mx_s[...]
        if old is not None:
            acc = acc_s[...]
        for p in range(WIDE // PIECE):
            at = slice(p * PIECE, (p + 1) * PIECE)
            if old is not None:
                w = jnp.exp2(s_s[zt, :, at] * SCALE - top).astype(jnp.bfloat16)
                acc = acc + dot(w, ve_s[zt, at, :])
            if new is not None:
                s = dot(q, k_s[zt, :, at])
                if masked:
                    n = iota((ROWS, PIECE), 1) + p * PIECE % TILE
                    r = iota((ROWS, PIECE), 0) % TOK
                    side = c if p * PIECE < TILE else 1 - c
                    k_pos = (n // CUT) * (2 * TOK) + n % CUT + side * TOK + u * CUT
                    s = jnp.where(k_pos <= r + (y * 2 + c) * TOK, s, LOW)
                s_s[zt, :, at] = s
                for i in range(PIECE // HD):
                    m = jnp.maximum(m, s[:, i * HD : (i + 1) * HD])
        if new is not None:
            mx_s[...] = m
        if old is not None:
            acc_s[...] = acc

    def sweep(new, old, top):
        if new is not None:
            mx_s[...] = jnp.full((ROWS, HD), LOW, jnp.float32)
        if old is not None:
            acc_s[...] = jnp.zeros((ROWS, 2 * HD), jnp.float32)

        def step(zt, _):
            body(zt, False, new, old, top)
            return 0

        lax.fori_loop(0, zh, step, 0)
        body(zh, True, new, old, top)

    def tops():
        return jnp.maximum(jnp.max(mx_s[...], axis=1, keepdims=True), FLOOR) * SCALE

    def finish(hh, top):
        total = acc_s[:, HD : 2 * HD]
        some = total > 0.0
        safe = jnp.where(some, total, 1.0)
        lse = jnp.where(some, top + jnp.log2(safe), LOW)
        hi = lse.astype(jnp.bfloat16).astype(jnp.float32)
        mid = (lse - hi).astype(jnp.bfloat16).astype(jnp.float32)
        lane = iota((ROWS, HD), 1) - 3 * hh
        parts = jnp.where(lane == 0, hi, jnp.where(lane == 1, mid, lse - hi - mid))
        return acc_s[:, 0:HD] / safe, parts

    sweep(0, None, None)
    top0 = tops()
    sweep(1, 0, top0)
    o0_s[...], st_s[...] = finish(0, top0)
    top1 = tops()
    sweep(None, 1, top1)
    o1, st1 = finish(1, top1)
    o0 = o0_s[...]
    lane = iota((ROWS, HD), 1)
    stats = jnp.where(lane < 3, st_s[...], st1)
    left = lane < HD // 2
    sides = (
        jnp.where(left, o0, pltpu.roll(o1, HD // 2, 1)).astype(jnp.bfloat16),
        jnp.where(left, pltpu.roll(o0, HD // 2, 1), o1).astype(jnp.bfloat16),
    )
    for i in range(NS):
        up = u + (1 - 2 * (u // 2)) * 2 * (i % 2) + (1 - 2 * (u % 2)) * (i // 2)
        rows = slice(i * TOK, (i + 1) * TOK)
        turned = jnp.transpose(stats[rows])
        tail = jnp.concatenate([turned[0:8, 0:HD], turned[0:8, HD : 2 * HD]], axis=0)
        for side in range(NC):
            o_ref[side * NS + up, 0:TOK, :] = sides[side][rows]
            o_ref[side * NS + up, TOK : TOK + STAT, :] = tail.astype(jnp.bfloat16)


def combine_kernel(r_ref, x_ref, many_ref):
    left = iota((HD, HD), 1) < HD // 2
    for half in range(2):
        shares = []
        for c in range(NC):
            for hh in range(2):
                lses = []
                for s in range(c * NS, (c + 1) * NS):
                    t = r_ref[s, TOK : TOK + STAT, :].astype(jnp.float32)
                    at = half * 8 + hh * 3
                    lses.append(t[at : at + 1] + t[at + 1 : at + 2] + t[at + 2 : at + 3])
                top = jnp.maximum(jnp.maximum(lses[0], lses[1]), jnp.maximum(lses[2], lses[3]))
                w = [jnp.exp2(lse - top) for lse in lses]
                inv = 1.0 / (w[0] + w[1] + w[2] + w[3])
                shares += [part * inv for part in w]
        shares.append(jnp.zeros((HD - len(shares), HD), jnp.float32))
        turned = jnp.transpose(jnp.concatenate(shares, axis=0))
        for c in range(NC):
            x = jnp.zeros((HD, HD), jnp.float32)
            for s in range(NS):
                at = c * 2 * NS + s
                w = jnp.where(left, turned[:, at : at + 1], turned[:, at + NS : at + NS + 1])
                x = x + r_ref[c * NS + s, half * HD : (half + 1) * HD, :].astype(jnp.float32) * w
            x = x.astype(jnp.bfloat16)
            rows = slice(c * TOK + half * HD, c * TOK + (half + 1) * HD)
            x_ref[rows, :] = x
            for i in range(8):
                many_ref[i, rows, :] = x


def assemble_kernel(pos_ref, own_ref, oth_ref, x_ref, out_ref):
    c = pos_ref[2]
    at, to = iota((HD, 2 * HD), 0), iota((HD, 2 * HD), 1)
    x = jnp.zeros((NC * TOK, 2 * HD), jnp.float32)
    for part_ref, side in ((own_ref, c), (oth_ref, 1 - c)):
        x = x + dot(part_ref[...], (to == column(side, at)).astype(jnp.bfloat16))
    x_ref[...] = x.astype(jnp.bfloat16)
    out_ref[...] = x_ref[pl.ds(pl.multiple_of(c * TOK, TOK), TOK), :]


def gram_kernel(r_ref, x_ref, h_ref):
    x = x_ref[...]
    for i in range(8):
        part = dot(r_ref[i], x, ATB)
        h_ref[i * 4 : (i + 1) * 4] = part.astype(jnp.bfloat16).reshape(4, 32, 2 * HD)


def call(kernel, name, outs, args, scratch=(), flops=0, moved=0):
    spaces = [pltpu.SMEM if a.dtype == jnp.int32 else pltpu.VMEM for a in args]
    shapes = [jax.ShapeDtypeStruct(s, jnp.bfloat16) for s in outs]
    return pl.pallas_call(
        kernel,
        out_shape=shapes,
        in_specs=[pl.BlockSpec(memory_space=s) for s in spaces],
        out_specs=[pl.BlockSpec(memory_space=pltpu.VMEM)] * len(outs),
        scratch_shapes=list(scratch),
        compiler_params=pltpu.CompilerParams(vmem_limit_bytes=40 << 20),
        cost_estimate=pl.CostEstimate(flops=flops, bytes_accessed=moved, transcendentals=0),
        name=name,
    )(*args)


def local(queries, keys, values):
    spots = [lax.axis_index(a) for a in CTX] + [lax.axis_index(SHARE), lax.axis_index("g")]
    pos = jnp.stack(spots).astype(jnp.int32)
    swap = [(0, 1), (1, 0)]
    (own,) = call(prep_kernel, "prep", [(NZ * NY, CUT, 2 * HD)], (pos, keys, values))
    with jax.named_scope("kv_gather"):
        kv_own = lax.all_to_all(own, CHIPS, 0, 0).reshape(KEYS, 2 * HD)
    with jax.named_scope("q_gather"):
        q1 = lax.ppermute(queries, "xl", swap)
        q2 = lax.ppermute(jnp.stack([queries, q1]), "zl", swap)
    with jax.named_scope("kv_swap"):
        kv_oth = lax.ppermute(kv_own, "c", swap)
    f32, bf16 = jnp.float32, jnp.bfloat16
    scratch = (
        pltpu.VMEM((2, ROWS, HD), bf16),
        pltpu.VMEM((NZ, HD, WIDE), bf16),
        pltpu.VMEM((NZ, WIDE, 2 * HD), bf16),
        pltpu.VMEM((NZ, ROWS, WIDE), f32),
        pltpu.VMEM((ROWS, HD), f32),
        pltpu.VMEM((ROWS, 2 * HD), f32),
        pltpu.VMEM((ROWS, HD), f32),
        pltpu.VMEM((ROWS, HD), f32),
    )
    (part,) = call(
        attend_kernel,
        "attend",
        [(NC * NS, TOK + STAT, HD)],
        (pos, queries, q1, q2, kv_own, kv_oth),
        scratch,
        flops=1 << 33,
    )
    with jax.named_scope("part_exchange"):
        parts = lax.all_to_all(part, ("c",) + SHARE, 0, 0)
    x_own, x_many = call(
        combine_kernel, "combine", [(NC * TOK, HD), (8, NC * TOK, HD)], (parts,)
    )
    with jax.named_scope("x_swap"):
        x_oth = lax.ppermute(x_own, "c", swap)
    with jax.named_scope("x_gather"):
        x_all = lax.all_to_all(x_many, HEAD, 0, 0)
    x, attn_out = call(
        assemble_kernel,
        "assemble",
        [(NC * TOK, 2 * HD), (TOK, 2 * HD)],
        (pos, x_own, x_oth),
        flops=1 << 27,
        moved=1 << 20,
    )
    (gram,) = call(gram_kernel, "gram", [(NZ * NY, 32, 2 * HD)], (x_all, x))
    with jax.named_scope("h_exchange"):
        h_parts = lax.all_to_all(gram, CHIPS, 0, 0)
    hessian = jnp.sum(h_parts.astype(jnp.float32), axis=0) * (2.0 / TOKENS)
    return attn_out, hessian


def solution(mesh):
    cut = Mesh(mesh.devices.reshape(NZ, NY, NC, 2, 2, 2), CTX + HEAD)
    in_specs = (P(CTX, HEAD), P(CTX, None), P(CTX, None))
    out_specs = (P(CTX, HEAD), P(CTX, HEAD))
    return jax.shard_map(local, mesh=cut, in_specs=in_specs, out_specs=out_specs, check_vma=False)
```

```python
import math

import jax
import jax.numpy as jnp
from jax import lax
from jax.experimental import pallas as pl
from jax.experimental.pallas import tpu as pltpu
from jax.sharding import Mesh
from jax.sharding import PartitionSpec as P

HEADS = 16
KVG = 2
HD = 128
TOKENS = 16384

CTX = ("zh", "yh", "b", "c")
HEAD = ("g", "xl", "zl")
CHIPS = ("zh", "yh", "b")
PAIRS = ("zh", "yh")
QUAD = ("b", "c")
SHARE = ("xl", "zl")
NZ, NY, NC, NS = 4, 8, 2, 4
NQ = 4
GRP = HD // NQ
TOK = 256
CUT = TOK // NS
TILE = NY * CUT
WIDE = NC * TILE
KEYS = NZ * TILE
ROWS = NS * TOK
PIECE = 256
SCALE = math.log2(math.e) / math.sqrt(HD)
LOW = -1e30
FLOOR = -1e29
STAT = 16
ABC = (((1,), (0,)), ((), ()))
ATB = (((0,), (0,)), ((), ()))


def dot(a, b, dims=ABC):
    return lax.dot_general(a, b, dims, preferred_element_type=jnp.float32)


def iota(shape, dim):
    return lax.broadcasted_iota(jnp.int32, shape, dim)


def spot(axes):
    return lax.axis_index(axes)


def prep_kernel(k_ref, v_ref, o_ref, kv_s, sems):
    rows = pl.ds(pl.multiple_of(spot(SHARE) * CUT, CUT), CUT)
    cols = pl.ds(pl.multiple_of(spot("g") * HD, HD), HD)
    copies = [
        pltpu.make_async_copy(ref.at[rows, cols], kv_s.at[i], sems.at[i])
        for i, ref in enumerate((k_ref, v_ref))
    ]
    for copy in copies:
        copy.start()
    for copy in copies:
        copy.wait()
    for i in range(NZ * NY):
        for a in range(2):
            o_ref[i, :, a * HD : (a + 1) * HD] = kv_s[a]


def attend_kernel(
    q0_ref, q1_ref, q2_ref, own_ref, oth_ref, o_ref, q_s, k_s, ve_s, s_s, mx_s, acc_s, st_s, o0_s
):
    zh, y, c, u = spot("zh"), spot(("yh", "b")), spot("c"), spot(SHARE)
    for zt in range(NZ):
        for a, kv_ref in enumerate((own_ref, oth_ref)):
            src = slice(zt * TILE, (zt + 1) * TILE)
            dst = slice(a * TILE, (a + 1) * TILE)
            k_s[zt, :, dst] = jnp.transpose(kv_ref[src, 0:HD])
            ve_s[zt, dst, 0:HD] = kv_ref[src, HD : 2 * HD]
            ve_s[zt, dst, HD : 2 * HD] = jnp.ones((TILE, HD), jnp.bfloat16)
    for hh in range(2):
        cols = slice(hh * HD, (hh + 1) * HD)
        for i, q in enumerate((q0_ref[:, cols], q1_ref[:, cols], q2_ref[0, :, cols], q2_ref[1, :, cols])):
            q_s[hh, i * TOK : (i + 1) * TOK, :] = q

    def body(zt, masked, new, old, top):
        if new is not None:
            q = q_s[new]
            m = mx_s[...]
        if old is not None:
            acc = acc_s[...]
        for p in range(WIDE // PIECE):
            at = slice(p * PIECE, (p + 1) * PIECE)
            if old is not None:
                w = jnp.exp2(s_s[zt, :, at] * SCALE - top).astype(jnp.bfloat16)
                acc = acc + dot(w, ve_s[zt, at, :])
            if new is not None:
                s = dot(q, k_s[zt, :, at])
                if masked:
                    n = iota((ROWS, PIECE), 1) + p * PIECE % TILE
                    r = iota((ROWS, PIECE), 0) % TOK
                    side = c if p * PIECE < TILE else 1 - c
                    k_pos = (n // CUT) * (2 * TOK) + n % CUT + side * TOK + u * CUT
                    s = jnp.where(k_pos <= r + (y * 2 + c) * TOK, s, LOW)
                s_s[zt, :, at] = s
                for i in range(PIECE // HD):
                    m = jnp.maximum(m, s[:, i * HD : (i + 1) * HD])
        if new is not None:
            mx_s[...] = m
        if old is not None:
            acc_s[...] = acc

    def sweep(new, old, top):
        if new is not None:
            mx_s[...] = jnp.full((ROWS, HD), LOW, jnp.float32)
        if old is not None:
            acc_s[...] = jnp.zeros((ROWS, 2 * HD), jnp.float32)

        def step(zt, _):
            body(zt, False, new, old, top)
            return 0

        lax.fori_loop(0, zh, step, 0)
        body(zh, True, new, old, top)

    def tops():
        return jnp.maximum(jnp.max(mx_s[...], axis=1, keepdims=True), FLOOR) * SCALE

    def finish(hh, top):
        total = acc_s[:, HD : 2 * HD]
        some = total > 0.0
        safe = jnp.where(some, total, 1.0)
        lse = jnp.where(some, top + jnp.log2(safe), LOW)
        hi = lse.astype(jnp.bfloat16).astype(jnp.float32)
        mid = (lse - hi).astype(jnp.bfloat16).astype(jnp.float32)
        lane = iota((ROWS, HD), 1) - 3 * hh
        parts = jnp.where(lane == 0, hi, jnp.where(lane == 1, mid, lse - hi - mid))
        return acc_s[:, 0:HD] / safe, parts

    sweep(0, None, None)
    top0 = tops()
    sweep(1, 0, top0)
    o0_s[...], st_s[...] = finish(0, top0)
    top1 = tops()
    sweep(None, 1, top1)
    o1, st1 = finish(1, top1)
    stats = jnp.where(iota((ROWS, HD), 1) < 3, st_s[...], st1)
    place = iota((TOK // 2, HD), 1) // GRP

    def swap(a, b, by):
        even = place // (by // GRP) % 2 == 0
        return (
            jnp.where(even, a, pltpu.roll(b, by, 1)),
            jnp.where(even, pltpu.roll(a, HD - by, 1), b),
        )

    for i in range(NS):
        up = u + (1 - 2 * (u // 2)) * 2 * (i % 2) + (1 - 2 * (u % 2)) * (i // 2)
        at = i * TOK
        mid, end = at + TOK // 2, at + TOK
        low0, low1 = swap(o0_s[at:mid], o1[at:mid], GRP)
        high0, high1 = swap(o0_s[mid:end], o1[mid:end], GRP)
        slots = [None] * NQ
        slots[0], slots[2] = swap(low0, high0, 2 * GRP)
        slots[1], slots[3] = swap(low1, high1, 2 * GRP)
        turned = jnp.transpose(stats[at:end])
        tail = jnp.concatenate([turned[0:8, 0:HD], turned[0:8, HD : 2 * HD]], axis=0)
        for k in range(NQ):
            o_ref[k * NS + up, 0:HD, :] = slots[k].astype(jnp.bfloat16)
            o_ref[k * NS + up, HD : HD + STAT, :] = tail.astype(jnp.bfloat16)


def combine_kernel(r_ref, x_ref, many_ref):
    place = iota((HD, HD), 1) // GRP
    turned = []
    for half in range(2):
        shares = []
        for k in range(NQ):
            for hh in range(2):
                lses = []
                for s in range(k * NS, (k + 1) * NS):
                    t = r_ref[s, HD : HD + STAT, :].astype(jnp.float32)
                    at = half * 8 + hh * 3
                    lses.append(t[at : at + 1] + t[at + 1 : at + 2] + t[at + 2 : at + 3])
                top = jnp.maximum(jnp.maximum(lses[0], lses[1]), jnp.maximum(lses[2], lses[3]))
                w = [jnp.exp2(lse - top) for lse in lses]
                inv = 1.0 / (w[0] + w[1] + w[2] + w[3])
                shares += [part * inv for part in w]
        shares.append(jnp.zeros((HD - len(shares), HD), jnp.float32))
        turned.append(jnp.transpose(jnp.concatenate(shares, axis=0)))
    for k in range(NQ):
        x = jnp.zeros((HD, HD), jnp.float32)
        for s in range(NS):
            at = k * 2 * NS + s
            w = [turned[i // 2][:, at + i % 2 * NS : at + i % 2 * NS + 1] for i in range(NQ)]
            w = jnp.where(place < 2, jnp.where(place == 0, w[0], w[1]), jnp.where(place == 2, w[2], w[3]))
            x = x + r_ref[k * NS + s, 0:HD, :].astype(jnp.float32) * w
        x = x.astype(jnp.bfloat16)
        rows = slice(k * HD, (k + 1) * HD)
        x_ref[rows, :] = x
        for i in range(8):
            many_ref[i, rows, :] = x


def assemble_kernel(x0_ref, x1_ref, x2_ref, x_ref, out_ref):
    b, c = spot("b"), spot("c")
    at, to = iota((HD, 2 * HD), 0), iota((HD, 2 * HD), 1)
    parts = ((x0_ref[...], b, c), (x1_ref[...], 1 - b, c), (x2_ref[0], b, 1 - c), (x2_ref[1], 1 - b, 1 - c))
    for half in range(2):
        x = jnp.zeros((NQ * HD, 2 * HD), jnp.float32)
        for part, pb, pc in parts:
            place = at - half * (HD // 2)
            col = place // GRP * HD + (pb * 2 + pc) * GRP + place % GRP
            pick = jnp.logical_and(at // (HD // 2) == half, to == col)
            x = x + dot(part, pick.astype(jnp.bfloat16))
        x_ref[half] = x.astype(jnp.bfloat16)
        mine = pl.ds(pl.multiple_of((b * 2 + c) * HD, HD), HD)
        out_ref[half * HD : (half + 1) * HD, :] = x_ref[half, mine, :]


def gram_kernel(r_ref, x_ref, h_ref):
    for i in range(8):
        part = dot(r_ref[i], x_ref[0], ATB)[0 : HD // 2] + dot(r_ref[i], x_ref[1], ATB)[HD // 2 : HD]
        h_ref[i * 2 : (i + 1) * 2] = part.astype(jnp.bfloat16).reshape(2, GRP, 2 * HD)


def call(kernel, name, outs, args, scratch=(), flops=0, moved=0, space=pltpu.VMEM, limit=40):
    return pl.pallas_call(
        kernel,
        out_shape=[jax.ShapeDtypeStruct(s, jnp.bfloat16) for s in outs],
        in_specs=[pl.BlockSpec(memory_space=space)] * len(args),
        out_specs=[pl.BlockSpec(memory_space=pltpu.VMEM)] * len(outs),
        scratch_shapes=list(scratch),
        compiler_params=pltpu.CompilerParams(vmem_limit_bytes=limit << 20),
        cost_estimate=pl.CostEstimate(flops=flops, bytes_accessed=moved, transcendentals=0),
        name=name,
    )(*args)


def local(queries, keys, values):
    swap = [(0, 1), (1, 0)]
    (own,) = call(
        prep_kernel,
        "prep",
        [(NZ * NY, CUT, 2 * HD)],
        (keys, values),
        (pltpu.VMEM((2, CUT, HD), jnp.bfloat16), pltpu.SemaphoreType.DMA((2,))),
        moved=1 << 20,
        space=pl.ANY,
        limit=60,
    )
    with jax.named_scope("q_gather"):
        q1 = lax.ppermute(queries, "xl", swap)
        q2 = lax.ppermute(jnp.stack([queries, q1]), "zl", swap)
    with jax.named_scope("kv_gather"):
        kv_own = lax.all_to_all(own, CHIPS, 0, 0)
        kv_own, q2 = lax.optimization_barrier((kv_own, q2))
        kv_own = kv_own.reshape(KEYS, 2 * HD)
    with jax.named_scope("kv_swap"):
        kv_oth = lax.ppermute(kv_own, "c", swap)
    f32, bf16 = jnp.float32, jnp.bfloat16
    scratch = (
        pltpu.VMEM((2, ROWS, HD), bf16),
        pltpu.VMEM((NZ, HD, WIDE), bf16),
        pltpu.VMEM((NZ, WIDE, 2 * HD), bf16),
        pltpu.VMEM((NZ, ROWS, WIDE), f32),
        pltpu.VMEM((ROWS, HD), f32),
        pltpu.VMEM((ROWS, 2 * HD), f32),
        pltpu.VMEM((ROWS, HD), f32),
        pltpu.VMEM((ROWS, HD), f32),
    )
    (part,) = call(
        attend_kernel,
        "attend",
        [(NQ * NS, HD + STAT, HD)],
        (queries, q1, q2, kv_own, kv_oth),
        scratch,
        flops=1 << 33,
    )
    with jax.named_scope("part_exchange"):
        parts = lax.all_to_all(part, QUAD + SHARE, 0, 0)
    x0, x_many = call(combine_kernel, "combine", [(NQ * HD, HD), (8, NQ * HD, HD)], (parts,))
    with jax.named_scope("x_swap"):
        x1 = lax.ppermute(x0, "b", swap)
        x2 = lax.ppermute(jnp.stack([x0, x1]), "c", swap)
    with jax.named_scope("x_gather"):
        x_all = lax.all_to_all(x_many, HEAD, 0, 0)
    x, attn_out = call(
        assemble_kernel,
        "assemble",
        [(2, NQ * HD, 2 * HD), (TOK, 2 * HD)],
        (x0, x1, x2),
        flops=1 << 28,
        moved=1 << 20,
    )
    (gram,) = call(gram_kernel, "gram", [(NZ * NY // 2, GRP, 2 * HD)], (x_all, x))
    with jax.named_scope("h_exchange"):
        h_parts = lax.all_to_all(gram, PAIRS, 0, 0)
    hessian = jnp.sum(h_parts.astype(jnp.float32), axis=0) * (2.0 / TOKENS)
    return attn_out, hessian


def solution(mesh):
    cut = Mesh(mesh.devices.reshape(NZ, NY // 2, 2, NC, 2, 2, 2), CTX + HEAD)
    in_specs = (P(CTX, HEAD), P(CTX, None), P(CTX, None))
    out_specs = (P(CTX, HEAD), P(CTX, HEAD))
    return jax.shard_map(local, mesh=cut, in_specs=in_specs, out_specs=out_specs, check_vma=False)
```

```python
import math

import jax
import jax.numpy as jnp
from jax import lax
from jax.experimental import pallas as pl
from jax.experimental.pallas import tpu as pltpu
from jax.sharding import Mesh
from jax.sharding import PartitionSpec as P

HEADS = 16
KVG = 2
HD = 128
TOKENS = 16384

CTX = ("zh", "yh", "b", "c")
HEAD = ("g", "xl", "zl")
CHIPS = ("zh", "yh", "b")
PAIRS = ("zh", "yh")
QUAD = ("b", "c")
SHARE = ("xl", "zl")
NZ, NY, NC, NS = 4, 8, 2, 4
NQ = 4
GRP = HD // NQ
TOK = 256
CUT = TOK // NS
TILE = NY * CUT
WIDE = NC * TILE
KEYS = NZ * TILE
ROWS = NS * TOK
PIECE = 256
SCALE = math.log2(math.e) / math.sqrt(HD)
LOW = -1e30
FLOOR = -1e29
STAT = 16
ABC = (((1,), (0,)), ((), ()))
ATB = (((0,), (0,)), ((), ()))


def dot(a, b, dims=ABC):
    return lax.dot_general(a, b, dims, preferred_element_type=jnp.float32)


def iota(shape, dim):
    return lax.broadcasted_iota(jnp.int32, shape, dim)


def spot(axes):
    return lax.axis_index(axes)


def prep_kernel(k_ref, v_ref, o_ref, kv_s, sems):
    rows = pl.ds(pl.multiple_of(spot(SHARE) * CUT, CUT), CUT)
    cols = pl.ds(pl.multiple_of(spot("g") * HD, HD), HD)
    copies = [
        pltpu.make_async_copy(ref.at[rows, cols], kv_s.at[i], sems.at[i])
        for i, ref in enumerate((k_ref, v_ref))
    ]
    for copy in copies:
        copy.start()
    for copy in copies:
        copy.wait()
    for i in range(NZ * NY):
        for a in range(2):
            o_ref[i, :, a * HD : (a + 1) * HD] = kv_s[a]


def attend_kernel(
    q0_ref, q1_ref, q2_ref, own_ref, oth_ref, o_ref, q_s, k_s, ve_s, s_s, mx_s, acc_s, st_s, o0_s
):
    zh, y, c, u = spot("zh"), spot(("yh", "b")), spot("c"), spot(SHARE)
    for zt in range(NZ):
        for a, kv_ref in enumerate((own_ref, oth_ref)):
            src = slice(zt * TILE, (zt + 1) * TILE)
            dst = slice(a * TILE, (a + 1) * TILE)
            k_s[zt, :, dst] = jnp.transpose(kv_ref[src, 0:HD])
            ve_s[zt, dst, 0:HD] = kv_ref[src, HD : 2 * HD]
            ve_s[zt, dst, HD : 2 * HD] = jnp.ones((TILE, HD), jnp.bfloat16)
    for hh in range(2):
        cols = slice(hh * HD, (hh + 1) * HD)
        for i, q in enumerate((q0_ref[:, cols], q1_ref[:, cols], q2_ref[0, :, cols], q2_ref[1, :, cols])):
            q_s[hh, i * TOK : (i + 1) * TOK, :] = q

    def body(zt, masked, new, old, top):
        if new is not None:
            q = q_s[new]
            m = mx_s[...]
        if old is not None:
            acc = acc_s[...]
        for p in range(WIDE // PIECE):
            at = slice(p * PIECE, (p + 1) * PIECE)
            if old is not None:
                w = jnp.exp2(s_s[zt, :, at] * SCALE - top).astype(jnp.bfloat16)
                acc = acc + dot(w, ve_s[zt, at, :])
            if new is not None:
                s = dot(q, k_s[zt, :, at])
                if masked:
                    n = iota((ROWS, PIECE), 1) + p * PIECE % TILE
                    r = iota((ROWS, PIECE), 0) % TOK
                    side = c if p * PIECE < TILE else 1 - c
                    k_pos = (n // CUT) * (2 * TOK) + n % CUT + side * TOK + u * CUT
                    s = jnp.where(k_pos <= r + (y * 2 + c) * TOK, s, LOW)
                s_s[zt, :, at] = s
                for i in range(PIECE // HD):
                    m = jnp.maximum(m, s[:, i * HD : (i + 1) * HD])
        if new is not None:
            mx_s[...] = m
        if old is not None:
            acc_s[...] = acc

    def sweep(new, old, top):
        if new is not None:
            mx_s[...] = jnp.full((ROWS, HD), LOW, jnp.float32)
        if old is not None:
            acc_s[...] = jnp.zeros((ROWS, 2 * HD), jnp.float32)

        def step(zt, _):
            body(zt, False, new, old, top)
            return 0

        lax.fori_loop(0, zh, step, 0)
        body(zh, True, new, old, top)

    def tops():
        return jnp.maximum(jnp.max(mx_s[...], axis=1, keepdims=True), FLOOR) * SCALE

    def finish(hh, top):
        total = acc_s[:, HD : 2 * HD]
        some = total > 0.0
        safe = jnp.where(some, total, 1.0)
        lse = jnp.where(some, top + jnp.log2(safe), LOW)
        hi = lse.astype(jnp.bfloat16).astype(jnp.float32)
        mid = (lse - hi).astype(jnp.bfloat16).astype(jnp.float32)
        lane = iota((ROWS, HD), 1) - 3 * hh
        parts = jnp.where(lane == 0, hi, jnp.where(lane == 1, mid, lse - hi - mid))
        return acc_s[:, 0:HD] / safe, parts

    sweep(0, None, None)
    top0 = tops()
    sweep(1, 0, top0)
    o0_s[...], st_s[...] = finish(0, top0)
    top1 = tops()
    sweep(None, 1, top1)
    o1, st1 = finish(1, top1)
    stats = jnp.where(iota((ROWS, HD), 1) < 3, st_s[...], st1)
    place = iota((TOK // 2, HD), 1) // GRP

    def swap(a, b, by):
        even = place // (by // GRP) % 2 == 0
        return (
            jnp.where(even, a, pltpu.roll(b, by, 1)),
            jnp.where(even, pltpu.roll(a, HD - by, 1), b),
        )

    for i in range(NS):
        up = u + (1 - 2 * (u // 2)) * 2 * (i % 2) + (1 - 2 * (u % 2)) * (i // 2)
        at = i * TOK
        mid, end = at + TOK // 2, at + TOK
        low0, low1 = swap(o0_s[at:mid], o1[at:mid], GRP)
        high0, high1 = swap(o0_s[mid:end], o1[mid:end], GRP)
        slots = [None] * NQ
        slots[0], slots[2] = swap(low0, high0, 2 * GRP)
        slots[1], slots[3] = swap(low1, high1, 2 * GRP)
        turned = jnp.transpose(stats[at:end])
        tail = jnp.concatenate([turned[0:8, 0:HD], turned[0:8, HD : 2 * HD]], axis=0)
        for k in range(NQ):
            o_ref[k * NS + up, 0:HD, :] = slots[k].astype(jnp.bfloat16)
            o_ref[k * NS + up, HD : HD + STAT, :] = tail.astype(jnp.bfloat16)


def combine_kernel(r_ref, x_ref, many_ref):
    row = iota((STAT, HD), 0)
    lanes = jnp.logical_and(row % NQ == iota((STAT, HD), 1) // GRP, row < 3 * NQ).astype(jnp.bfloat16)
    for k in range(NQ):
        shares = [[] for _ in range(NS)]
        for place in range(NQ):
            lses = []
            for s in range(k * NS, (k + 1) * NS):
                at = HD + place // 2 * 8 + place % 2 * 3
                t = r_ref[s, HD : HD + STAT, :].astype(jnp.float32)[at - HD : at - HD + 3]
                lses.append(t[0:1] + t[1:2] + t[2:3])
            top = jnp.maximum(jnp.maximum(lses[0], lses[1]), jnp.maximum(lses[2], lses[3]))
            w = [jnp.exp2(lse - top) for lse in lses]
            inv = 1.0 / (w[0] + w[1] + w[2] + w[3])
            for s in range(NS):
                shares[s].append(w[s] * inv)
        x = jnp.zeros((HD, HD), jnp.float32)
        for s in range(NS):
            w = jnp.concatenate(shares[s], axis=0)
            hi = w.astype(jnp.bfloat16).astype(jnp.float32)
            mid = (w - hi).astype(jnp.bfloat16).astype(jnp.float32)
            lever = jnp.concatenate([hi, mid, w - hi - mid, jnp.zeros_like(w)], axis=0)
            w = dot(lever.astype(jnp.bfloat16), lanes, ATB)
            x = x + r_ref[k * NS + s, 0:HD, :].astype(jnp.float32) * w
        x = x.astype(jnp.bfloat16)
        rows = slice(k * HD, (k + 1) * HD)
        x_ref[rows, :] = x
        for i in range(8):
            many_ref[i, rows, :] = x


def assemble_kernel(x0_ref, x1_ref, x2_ref, x_ref, out_ref):
    b, c = spot("b"), spot("c")
    at, to = iota((HD, 2 * HD), 0), iota((HD, 2 * HD), 1)
    parts = ((x0_ref[...], b, c), (x1_ref[...], 1 - b, c), (x2_ref[0], b, 1 - c), (x2_ref[1], 1 - b, 1 - c))
    for half in range(2):
        x = jnp.zeros((NQ * HD, 2 * HD), jnp.float32)
        for part, pb, pc in parts:
            place = at - half * (HD // 2)
            col = place // GRP * HD + (pb * 2 + pc) * GRP + place % GRP
            pick = jnp.logical_and(at // (HD // 2) == half, to == col)
            x = x + dot(part, pick.astype(jnp.bfloat16))
        x_ref[half] = x.astype(jnp.bfloat16)
        mine = pl.ds(pl.multiple_of((b * 2 + c) * HD, HD), HD)
        out_ref[half * HD : (half + 1) * HD, :] = x_ref[half, mine, :]


def gram_kernel(r_ref, x_ref, h_ref):
    for i in range(8):
        part = dot(r_ref[i], x_ref[0], ATB)[0 : HD // 2] + dot(r_ref[i], x_ref[1], ATB)[HD // 2 : HD]
        h_ref[i * 2 : (i + 1) * 2] = part.astype(jnp.bfloat16).reshape(2, GRP, 2 * HD)


def call(kernel, name, outs, args, scratch=(), flops=0, moved=0, space=pltpu.VMEM, limit=40):
    return pl.pallas_call(
        kernel,
        out_shape=[jax.ShapeDtypeStruct(s, jnp.bfloat16) for s in outs],
        in_specs=[pl.BlockSpec(memory_space=space)] * len(args),
        out_specs=[pl.BlockSpec(memory_space=pltpu.VMEM)] * len(outs),
        scratch_shapes=list(scratch),
        compiler_params=pltpu.CompilerParams(vmem_limit_bytes=limit << 20),
        cost_estimate=pl.CostEstimate(flops=flops, bytes_accessed=moved, transcendentals=0),
        name=name,
    )(*args)


def local(queries, keys, values):
    swap = [(0, 1), (1, 0)]
    (own,) = call(
        prep_kernel,
        "prep",
        [(NZ * NY, CUT, 2 * HD)],
        (keys, values),
        (pltpu.VMEM((2, CUT, HD), jnp.bfloat16), pltpu.SemaphoreType.DMA((2,))),
        moved=1 << 20,
        space=pl.ANY,
        limit=60,
    )
    with jax.named_scope("q_gather"):
        q1 = lax.ppermute(queries, "xl", swap)
        q2 = lax.ppermute(jnp.stack([queries, q1]), "zl", swap)
    with jax.named_scope("kv_gather"):
        kv_own = lax.all_to_all(own, CHIPS, 0, 0)
        kv_own, q2 = lax.optimization_barrier((kv_own, q2))
        kv_own = kv_own.reshape(KEYS, 2 * HD)
    with jax.named_scope("kv_swap"):
        kv_oth = lax.ppermute(kv_own, "c", swap)
    f32, bf16 = jnp.float32, jnp.bfloat16
    scratch = (
        pltpu.VMEM((2, ROWS, HD), bf16),
        pltpu.VMEM((NZ, HD, WIDE), bf16),
        pltpu.VMEM((NZ, WIDE, 2 * HD), bf16),
        pltpu.VMEM((NZ, ROWS, WIDE), f32),
        pltpu.VMEM((ROWS, HD), f32),
        pltpu.VMEM((ROWS, 2 * HD), f32),
        pltpu.VMEM((ROWS, HD), f32),
        pltpu.VMEM((ROWS, HD), f32),
    )
    (part,) = call(
        attend_kernel,
        "attend",
        [(NQ * NS, HD + STAT, HD)],
        (queries, q1, q2, kv_own, kv_oth),
        scratch,
        flops=1 << 33,
    )
    with jax.named_scope("part_exchange"):
        parts = lax.all_to_all(part, QUAD + SHARE, 0, 0)
    x0, x_many = call(combine_kernel, "combine", [(NQ * HD, HD), (8, NQ * HD, HD)], (parts,))
    with jax.named_scope("x_swap"):
        x1 = lax.ppermute(x0, "b", swap)
        x2 = lax.ppermute(jnp.stack([x0, x1]), "c", swap)
    with jax.named_scope("x_gather"):
        x_all = lax.all_to_all(x_many, HEAD, 0, 0)
    x, attn_out = call(
        assemble_kernel,
        "assemble",
        [(2, NQ * HD, 2 * HD), (TOK, 2 * HD)],
        (x0, x1, x2),
        flops=1 << 28,
        moved=1 << 20,
    )
    (gram,) = call(gram_kernel, "gram", [(NZ * NY // 2, GRP, 2 * HD)], (x_all, x))
    with jax.named_scope("h_exchange"):
        h_parts = lax.all_to_all(gram, PAIRS, 0, 0)
    hessian = jnp.sum(h_parts.astype(jnp.float32), axis=0) * (2.0 / TOKENS)
    return attn_out, hessian


def solution(mesh):
    cut = Mesh(mesh.devices.reshape(NZ, NY // 2, 2, NC, 2, 2, 2), CTX + HEAD)
    in_specs = (P(CTX, HEAD), P(CTX, None), P(CTX, None))
    out_specs = (P(CTX, HEAD), P(CTX, HEAD))
    return jax.shard_map(local, mesh=cut, in_specs=in_specs, out_specs=out_specs, check_vma=False)
```

```python
import math

import jax
import jax.numpy as jnp
from jax import lax
from jax.experimental import pallas as pl
from jax.experimental.pallas import tpu as pltpu
from jax.sharding import Mesh
from jax.sharding import PartitionSpec as P

HEADS = 16
KVG = 2
HD = 128
TOKENS = 16384

CTX = ("zh", "yh", "b", "c")
HEAD = ("g", "xl", "zl")
CHIPS = ("zh", "yh", "b")
PAIRS = ("zh", "yh")
QUAD = ("b", "c")
SHARE = ("b", "xl")
NZ, NY, NC, NS = 4, 8, 2, 4
NQ = 4
GRP = HD // NQ
TOK = 256
CUT = TOK // NS
TILE = NY * CUT
WIDE = NC * TILE
KEYS = NZ * TILE
ROWS = NS * TOK
PIECE = 256
SCALE = math.log2(math.e) / math.sqrt(HD)
LOW = -1e30
FLOOR = -1e29
STAT = 16
ABC = (((1,), (0,)), ((), ()))
ATB = (((0,), (0,)), ((), ()))


def dot(a, b, dims=ABC):
    return lax.dot_general(a, b, dims, preferred_element_type=jnp.float32)


def iota(shape, dim):
    return lax.broadcasted_iota(jnp.int32, shape, dim)


def spot(axes):
    return lax.axis_index(axes)


def prep_kernel(k_ref, v_ref, o_ref, kv_s, sems):
    cols = pl.ds(pl.multiple_of(spot("g") * HD, HD), HD)
    copies = []
    for b in range(2):
        rows = pl.ds(pl.multiple_of((b * 2 + spot("xl")) * CUT, CUT), CUT)
        for i, ref in enumerate((k_ref, v_ref)):
            copies.append(pltpu.make_async_copy(ref.at[rows, cols], kv_s.at[b, i], sems.at[b, i]))
    for copy in copies:
        copy.start()
    for copy in copies:
        copy.wait()
    for i in range(NZ * NY):
        for a in range(2):
            o_ref[i, :, a * HD : (a + 1) * HD] = kv_s[i % 2, a]


def attend_kernel(
    q0_ref, q1_ref, q2_ref, own_ref, oth_ref, o_ref, q_s, k_s, ve_s, s_s, mx_s, acc_s, st_s, o0_s
):
    zh, yh, b, c, u, xl = spot("zh"), spot("yh"), spot("b"), spot("c"), spot(SHARE), spot("xl")
    for zt in range(NZ):
        for a, kv_ref in enumerate((own_ref, oth_ref)):
            src = slice(zt * TILE, (zt + 1) * TILE)
            dst = slice(a * TILE, (a + 1) * TILE)
            k_s[zt, :, dst] = jnp.transpose(kv_ref[src, 0:HD])
            ve_s[zt, dst, 0:HD] = kv_ref[src, HD : 2 * HD]
            ve_s[zt, dst, HD : 2 * HD] = jnp.ones((TILE, HD), jnp.bfloat16)
    for hh in range(2):
        cols = slice(hh * HD, (hh + 1) * HD)
        for i, q in enumerate((q0_ref[:, cols], q1_ref[:, cols], q2_ref[0, :, cols], q2_ref[1, :, cols])):
            q_s[hh, i * TOK : (i + 1) * TOK, :] = q

    def body(zt, masked, new, old, top):
        if new is not None:
            q = q_s[new]
            m = mx_s[...]
        if old is not None:
            acc = acc_s[...]
        for p in range(WIDE // PIECE):
            at = slice(p * PIECE, (p + 1) * PIECE)
            if old is not None:
                w = jnp.exp2(s_s[zt, :, at] * SCALE - top).astype(jnp.bfloat16)
                acc = acc + dot(w, ve_s[zt, at, :])
            if new is not None:
                s = dot(q, k_s[zt, :, at])
                if masked:
                    n = iota((ROWS, PIECE), 1) + p * PIECE % TILE
                    r = iota((ROWS, PIECE), 0)
                    r = r % TOK + jnp.where(r // (2 * TOK) == 0, b, 1 - b) * (NC * TOK)
                    side = c if p * PIECE < TILE else 1 - c
                    k_pos = (n // CUT) * (2 * TOK) + n % CUT + side * TOK + u * CUT
                    s = jnp.where(k_pos <= r + (yh * 2 * NC + c) * TOK, s, LOW)
                s_s[zt, :, at] = s
                for i in range(PIECE // HD):
                    m = jnp.maximum(m, s[:, i * HD : (i + 1) * HD])
        if new is not None:
            mx_s[...] = m
        if old is not None:
            acc_s[...] = acc

    def sweep(new, old, top):
        if new is not None:
            mx_s[...] = jnp.full((ROWS, HD), LOW, jnp.float32)
        if old is not None:
            acc_s[...] = jnp.zeros((ROWS, 2 * HD), jnp.float32)

        def step(zt, _):
            body(zt, False, new, old, top)
            return 0

        lax.fori_loop(0, zh, step, 0)
        body(zh, True, new, old, top)

    def tops():
        return jnp.maximum(jnp.max(mx_s[...], axis=1, keepdims=True), FLOOR) * SCALE

    def finish(hh, top):
        total = acc_s[:, HD : 2 * HD]
        some = total > 0.0
        safe = jnp.where(some, total, 1.0)
        lse = jnp.where(some, top + jnp.log2(safe), LOW)
        hi = lse.astype(jnp.bfloat16).astype(jnp.float32)
        mid = (lse - hi).astype(jnp.bfloat16).astype(jnp.float32)
        lane = iota((ROWS, HD), 1) - 3 * hh
        parts = jnp.where(lane == 0, hi, jnp.where(lane == 1, mid, lse - hi - mid))
        return acc_s[:, 0:HD] / safe, parts

    sweep(0, None, None)
    top0 = tops()
    sweep(1, 0, top0)
    o0_s[...], st_s[...] = finish(0, top0)
    top1 = tops()
    sweep(None, 1, top1)
    o1, st1 = finish(1, top1)
    stats = jnp.where(iota((ROWS, HD), 1) < 3, st_s[...], st1)
    place = iota((TOK // 2, HD), 1) // GRP

    def swap(a, b, by):
        even = place // (by // GRP) % 2 == 0
        return (
            jnp.where(even, a, pltpu.roll(b, by, 1)),
            jnp.where(even, pltpu.roll(a, HD - by, 1), b),
        )

    for i in range(NS):
        to_x = xl + (1 - 2 * xl) * (i % 2)
        to_b = b + (1 - 2 * b) * (i // 2)
        rows = pl.ds(pl.multiple_of(to_b * HD, HD), HD)
        tails = pl.ds(pl.multiple_of(2 * HD + to_b * STAT, STAT), STAT)
        at = i * TOK
        mid, end = at + TOK // 2, at + TOK
        low0, low1 = swap(o0_s[at:mid], o1[at:mid], GRP)
        high0, high1 = swap(o0_s[mid:end], o1[mid:end], GRP)
        slots = [None] * NQ
        slots[0], slots[2] = swap(low0, high0, 2 * GRP)
        slots[1], slots[3] = swap(low1, high1, 2 * GRP)
        turned = jnp.transpose(stats[at:end])
        tail = jnp.concatenate([turned[0:8, 0:HD], turned[0:8, HD : 2 * HD]], axis=0)
        for k in range(NQ):
            o_ref[k * 2 + to_x, rows, :] = slots[k].astype(jnp.bfloat16)
            o_ref[k * 2 + to_x, tails, :] = tail.astype(jnp.bfloat16)


def combine_kernel(r_ref, x_ref, many_ref):
    row = iota((STAT, HD), 0)
    lanes = jnp.logical_and(row % NQ == iota((STAT, HD), 1) // GRP, row < 3 * NQ).astype(jnp.bfloat16)
    for k in range(NQ):
        sources = [(s // 2 * NC + k % NC) * 2 + s % 2 for s in range(NS)]
        first, stat = k // NC * HD, 2 * HD + k // NC * STAT
        shares = [[] for _ in range(NS)]
        for place in range(NQ):
            lses = []
            for s in sources:
                at = place // 2 * 8 + place % 2 * 3
                t = r_ref[s, stat : stat + STAT, :].astype(jnp.float32)[at : at + 3]
                lses.append(t[0:1] + t[1:2] + t[2:3])
            top = jnp.maximum(jnp.maximum(lses[0], lses[1]), jnp.maximum(lses[2], lses[3]))
            w = [jnp.exp2(lse - top) for lse in lses]
            inv = 1.0 / (w[0] + w[1] + w[2] + w[3])
            for s in range(NS):
                shares[s].append(w[s] * inv)
        x = jnp.zeros((HD, HD), jnp.float32)
        for s in range(NS):
            w = jnp.concatenate(shares[s], axis=0)
            hi = w.astype(jnp.bfloat16).astype(jnp.float32)
            mid = (w - hi).astype(jnp.bfloat16).astype(jnp.float32)
            lever = jnp.concatenate([hi, mid, w - hi - mid, jnp.zeros_like(w)], axis=0)
            w = dot(lever.astype(jnp.bfloat16), lanes, ATB)
            x = x + r_ref[sources[s], first : first + HD, :].astype(jnp.float32) * w
        x = x.astype(jnp.bfloat16)
        rows = slice(k * HD, (k + 1) * HD)
        x_ref[rows, :] = x
        for i in range(8):
            many_ref[i, rows, :] = x


def assemble_kernel(x0_ref, x1_ref, x2_ref, x_ref, out_ref):
    b, c = spot("b"), spot("c")
    at, to = iota((HD, 2 * HD), 0), iota((HD, 2 * HD), 1)
    parts = ((x0_ref[...], b, c), (x1_ref[...], 1 - b, c), (x2_ref[0], b, 1 - c), (x2_ref[1], 1 - b, 1 - c))
    for half in range(2):
        x = jnp.zeros((NQ * HD, 2 * HD), jnp.float32)
        for part, pb, pc in parts:
            place = at - half * (HD // 2)
            col = place // GRP * HD + (pb * 2 + pc) * GRP + place % GRP
            pick = jnp.logical_and(at // (HD // 2) == half, to == col)
            x = x + dot(part, pick.astype(jnp.bfloat16))
        x_ref[half] = x.astype(jnp.bfloat16)
        mine = pl.ds(pl.multiple_of((b * 2 + c) * HD, HD), HD)
        out_ref[half * HD : (half + 1) * HD, :] = x_ref[half, mine, :]


def gram_kernel(r_ref, x_ref, h_ref):
    for i in range(8):
        part = dot(r_ref[i], x_ref[0], ATB)[0 : HD // 2] + dot(r_ref[i], x_ref[1], ATB)[HD // 2 : HD]
        h_ref[i * 2 : (i + 1) * 2] = part.astype(jnp.bfloat16).reshape(2, GRP, 2 * HD)


def call(kernel, name, outs, args, scratch=(), flops=0, moved=0, space=pltpu.VMEM, limit=40):
    return pl.pallas_call(
        kernel,
        out_shape=[jax.ShapeDtypeStruct(s, jnp.bfloat16) for s in outs],
        in_specs=[pl.BlockSpec(memory_space=space)] * len(args),
        out_specs=[pl.BlockSpec(memory_space=pltpu.VMEM)] * len(outs),
        scratch_shapes=list(scratch),
        compiler_params=pltpu.CompilerParams(vmem_limit_bytes=limit << 20),
        cost_estimate=pl.CostEstimate(flops=flops, bytes_accessed=moved, transcendentals=0),
        name=name,
    )(*args)


def local(queries, keys, values):
    swap = [(0, 1), (1, 0)]
    (own,) = call(
        prep_kernel,
        "prep",
        [(NZ * NY, CUT, 2 * HD)],
        (keys, values),
        (pltpu.VMEM((2, 2, CUT, HD), jnp.bfloat16), pltpu.SemaphoreType.DMA((2, 2))),
        moved=1 << 20,
        space=pl.ANY,
        limit=60,
    )
    with jax.named_scope("q_gather"):
        q1 = lax.ppermute(queries, "xl", swap)
        q2 = lax.ppermute(jnp.stack([queries, q1]), "b", swap)
    with jax.named_scope("kv_gather"):
        kv_own = lax.all_to_all(own, CHIPS, 0, 0)
        kv_own, q2 = lax.optimization_barrier((kv_own, q2))
        kv_own = kv_own.reshape(KEYS, 2 * HD)
    with jax.named_scope("kv_swap"):
        kv_oth = lax.ppermute(kv_own, "c", swap)
    f32, bf16 = jnp.float32, jnp.bfloat16
    scratch = (
        pltpu.VMEM((2, ROWS, HD), bf16),
        pltpu.VMEM((NZ, HD, WIDE), bf16),
        pltpu.VMEM((NZ, WIDE, 2 * HD), bf16),
        pltpu.VMEM((NZ, ROWS, WIDE), f32),
        pltpu.VMEM((ROWS, HD), f32),
        pltpu.VMEM((ROWS, 2 * HD), f32),
        pltpu.VMEM((ROWS, HD), f32),
        pltpu.VMEM((ROWS, HD), f32),
    )
    (part,) = call(
        attend_kernel,
        "attend",
        [(NQ * 2, 2 * (HD + STAT), HD)],
        (queries, q1, q2, kv_own, kv_oth),
        scratch,
        flops=1 << 33,
    )
    with jax.named_scope("part_exchange"):
        parts = lax.all_to_all(part, QUAD + ("xl",), 0, 0)
    x0, x_many = call(combine_kernel, "combine", [(NQ * HD, HD), (8, NQ * HD, HD)], (parts,))
    with jax.named_scope("x_swap"):
        x1 = lax.ppermute(x0, "b", swap)
        x2 = lax.ppermute(jnp.stack([x0, x1]), "c", swap)
    with jax.named_scope("x_gather"):
        x_all = lax.all_to_all(x_many, HEAD, 0, 0)
    x, attn_out = call(
        assemble_kernel,
        "assemble",
        [(2, NQ * HD, 2 * HD), (TOK, 2 * HD)],
        (x0, x1, x2),
        flops=1 << 28,
        moved=1 << 20,
    )
    (gram,) = call(gram_kernel, "gram", [(NZ * NY // 2, GRP, 2 * HD)], (x_all, x))
    with jax.named_scope("h_exchange"):
        h_parts = lax.all_to_all(gram, PAIRS, 0, 0)
    hessian = jnp.sum(h_parts.astype(jnp.float32), axis=0) * (2.0 / TOKENS)
    return attn_out, hessian


def solution(mesh):
    cut = Mesh(mesh.devices.reshape(NZ, NY // 2, 2, NC, 2, 2, 2), CTX + HEAD)
    in_specs = (P(CTX, HEAD), P(CTX, None), P(CTX, None))
    out_specs = (P(CTX, HEAD), P(CTX, HEAD))
    return jax.shard_map(local, mesh=cut, in_specs=in_specs, out_specs=out_specs, check_vma=False)
```

```python
import math

import jax
import jax.numpy as jnp
from jax import lax
from jax.experimental import pallas as pl
from jax.experimental.pallas import tpu as pltpu
from jax.sharding import Mesh
from jax.sharding import PartitionSpec as P

HEADS = 16
KVG = 2
HD = 128
TOKENS = 16384

CTX = ("zh", "yh", "b", "c")
HEAD = ("g", "xl", "zl")
CHIPS = ("zh", "yh", "b")
PAIRS = ("zh", "yh")
QUAD = ("b", "c")
SHARE = ("b", "xl")
NZ, NY, NC, NS = 4, 8, 2, 4
NQ = 4
GRP = HD // NQ
TOK = 256
CUT = TOK // NS
TILE = NY * CUT
KEYS = NZ * TILE
ROWS = NS * TOK
PIECE = 256
PIECES = TILE // PIECE
SCALE = math.log2(math.e) / math.sqrt(HD)
LOW = -1e30
FLOOR = -1e29
STAT = 16
ABC = (((1,), (0,)), ((), ()))
ATB = (((0,), (0,)), ((), ()))


def dot(a, b, dims=ABC):
    return lax.dot_general(a, b, dims, preferred_element_type=jnp.float32)


def iota(shape, dim):
    return lax.broadcasted_iota(jnp.int32, shape, dim)


def spot(axes):
    return lax.axis_index(axes)


def prep_kernel(k_ref, v_ref, o_ref, kv_s, sems):
    cols = pl.ds(pl.multiple_of(spot("g") * HD, HD), HD)
    copies = []
    for b in range(2):
        rows = pl.ds(pl.multiple_of((b * 2 + spot("xl")) * CUT, CUT), CUT)
        for i, ref in enumerate((k_ref, v_ref)):
            copies.append(pltpu.make_async_copy(ref.at[rows, cols], kv_s.at[b, i], sems.at[b, i]))
    for copy in copies:
        copy.start()
    for copy in copies:
        copy.wait()
    for i in range(NZ * NY):
        for a in range(2):
            o_ref[i, :, a * HD : (a + 1) * HD] = kv_s[i % 2, a]


def lay_keys(kv_ref, k_ref, ve_ref):
    for zt in range(NZ):
        src = slice(zt * TILE, (zt + 1) * TILE)
        k_ref[zt] = jnp.transpose(kv_ref[src, 0:HD])
        ve_ref[zt, :, 0:HD] = kv_ref[src, HD : 2 * HD]
        ve_ref[zt, :, HD : 2 * HD] = jnp.ones((TILE, HD), jnp.bfloat16)


def score(q, k_ref, zt, p, side, masked):
    s = dot(q, k_ref[zt, :, p * PIECE : (p + 1) * PIECE])
    if masked:
        b, c = spot("b"), spot("c")
        n = iota((ROWS, PIECE), 1) + p * PIECE
        r = iota((ROWS, PIECE), 0)
        r = r % TOK + jnp.where(r // (2 * TOK) == 0, b, 1 - b) * (NC * TOK)
        k_pos = (n // CUT) * (2 * TOK) + n % CUT + side * TOK + spot(SHARE) * CUT
        s = jnp.where(k_pos <= r + (spot("yh") * 2 * NC + c) * TOK, s, LOW)
    return s


def highest(m, s):
    for i in range(PIECE // HD):
        m = jnp.maximum(m, s[:, i * HD : (i + 1) * HD])
    return m


def begin_kernel(near_ref, far_ref, kv_ref, q_ref, k_ref, ve_ref, s_ref, mx_ref):
    lay_keys(kv_ref, k_ref, ve_ref)
    for hh in range(2):
        for i in range(NS):
            part_ref = (near_ref, far_ref)[i // 2]
            q_ref[hh, i * TOK : (i + 1) * TOK, :] = part_ref[i % 2, :, hh * HD : (hh + 1) * HD]
    mx_ref[...] = jnp.full((ROWS, HD), LOW, jnp.float32)

    def body(zt, masked):
        q = q_ref[0]
        m = mx_ref[...]
        for p in range(PIECES):
            s = score(q, k_ref, zt, p, spot("c"), masked)
            s_ref[zt, :, p * PIECE : (p + 1) * PIECE] = s
            m = highest(m, s)
        mx_ref[...] = m

    lax.fori_loop(0, spot("zh"), lambda zt, _: (body(zt, False), 0)[1], 0)
    body(spot("zh"), True)


def attend_kernel(
    q_ref, k0_ref, ve0_ref, s0_ref, mx0_ref, oth_ref, o_ref, k1_s, ve1_s, s_s, mx_s, acc_s, st_s, o0_s
):
    zh, b, c, xl = spot("zh"), spot("b"), spot("c"), spot("xl")
    lay_keys(oth_ref, k1_s, ve1_s)
    sides = ((k0_ref, ve0_ref, c), (k1_s, ve1_s, 1 - c))

    def body(zt, masked, new, old, top):
        if new is not None:
            q = q_ref[new]
            m = mx_s[...]
        if old is not None:
            acc = acc_s[...]
        for a, (k_ref, ve_ref, side) in enumerate(sides):
            for p in range(PIECES):
                at = slice(p * PIECE, (p + 1) * PIECE)
                if old is not None:
                    s_ref = s0_ref if old == 0 and a == 0 else s_s.at[a]
                    w = jnp.exp2(s_ref[zt, :, at] * SCALE - top).astype(jnp.bfloat16)
                    acc = acc + dot(w, ve_ref[zt, at, :])
                if new == 1 or new == 0 and a == 1:
                    s = score(q, k_ref, zt, p, side, masked)
                    s_s[a, zt, :, at] = s
                    m = highest(m, s)
        if new is not None:
            mx_s[...] = m
        if old is not None:
            acc_s[...] = acc

    def sweep(new, old, top):
        if new is not None:
            mx_s[...] = jnp.full((ROWS, HD), LOW, jnp.float32) if new else mx0_ref[...]
        if old is not None:
            acc_s[...] = jnp.zeros((ROWS, 2 * HD), jnp.float32)

        def step(zt, _):
            body(zt, False, new, old, top)
            return 0

        lax.fori_loop(0, zh, step, 0)
        body(zh, True, new, old, top)

    def tops():
        return jnp.maximum(jnp.max(mx_s[...], axis=1, keepdims=True), FLOOR) * SCALE

    def finish(hh, top):
        total = acc_s[:, HD : 2 * HD]
        some = total > 0.0
        safe = jnp.where(some, total, 1.0)
        lse = jnp.where(some, top + jnp.log2(safe), LOW)
        hi = lse.astype(jnp.bfloat16).astype(jnp.float32)
        mid = (lse - hi).astype(jnp.bfloat16).astype(jnp.float32)
        lane = iota((ROWS, HD), 1) - 3 * hh
        parts = jnp.where(lane == 0, hi, jnp.where(lane == 1, mid, lse - hi - mid))
        return acc_s[:, 0:HD] / safe, parts

    sweep(0, None, None)
    top0 = tops()
    sweep(1, 0, top0)
    o0_s[...], st_s[...] = finish(0, top0)
    top1 = tops()
    sweep(None, 1, top1)
    o1, st1 = finish(1, top1)
    stats = jnp.where(iota((ROWS, HD), 1) < 3, st_s[...], st1)
    place = iota((TOK // 2, HD), 1) // GRP

    def swap(a, b, by):
        even = place // (by // GRP) % 2 == 0
        return (
            jnp.where(even, a, pltpu.roll(b, by, 1)),
            jnp.where(even, pltpu.roll(a, HD - by, 1), b),
        )

    for i in range(NS):
        to_x = xl + (1 - 2 * xl) * (i % 2)
        to_b = b + (1 - 2 * b) * (i // 2)
        rows = pl.ds(pl.multiple_of(to_b * HD, HD), HD)
        tails = pl.ds(pl.multiple_of(2 * HD + to_b * STAT, STAT), STAT)
        at = i * TOK
        mid, end = at + TOK // 2, at + TOK
        low0, low1 = swap(o0_s[at:mid], o1[at:mid], GRP)
        high0, high1 = swap(o0_s[mid:end], o1[mid:end], GRP)
        slots = [None] * NQ
        slots[0], slots[2] = swap(low0, high0, 2 * GRP)
        slots[1], slots[3] = swap(low1, high1, 2 * GRP)
        turned = jnp.transpose(stats[at:end])
        tail = jnp.concatenate([turned[0:8, 0:HD], turned[0:8, HD : 2 * HD]], axis=0)
        for k in range(NQ):
            o_ref[k * 2 + to_x, rows, :] = slots[k].astype(jnp.bfloat16)
            o_ref[k * 2 + to_x, tails, :] = tail.astype(jnp.bfloat16)


def combine_kernel(r_ref, x_ref, many_ref):
    row = iota((STAT, HD), 0)
    lanes = jnp.logical_and(row % NQ == iota((STAT, HD), 1) // GRP, row < 3 * NQ).astype(jnp.bfloat16)
    for k in range(NQ):
        sources = [(s // 2 * NC + k % NC) * 2 + s % 2 for s in range(NS)]
        first, stat = k // NC * HD, 2 * HD + k // NC * STAT
        shares = [[] for _ in range(NS)]
        for place in range(NQ):
            lses = []
            for s in sources:
                at = place // 2 * 8 + place % 2 * 3
                t = r_ref[s, stat : stat + STAT, :].astype(jnp.float32)[at : at + 3]
                lses.append(t[0:1] + t[1:2] + t[2:3])
            top = jnp.maximum(jnp.maximum(lses[0], lses[1]), jnp.maximum(lses[2], lses[3]))
            w = [jnp.exp2(lse - top) for lse in lses]
            inv = 1.0 / (w[0] + w[1] + w[2] + w[3])
            for s in range(NS):
                shares[s].append(w[s] * inv)
        x = jnp.zeros((HD, HD), jnp.float32)
        for s in range(NS):
            w = jnp.concatenate(shares[s], axis=0)
            hi = w.astype(jnp.bfloat16).astype(jnp.float32)
            mid = (w - hi).astype(jnp.bfloat16).astype(jnp.float32)
            lever = jnp.concatenate([hi, mid, w - hi - mid, jnp.zeros_like(w)], axis=0)
            w = dot(lever.astype(jnp.bfloat16), lanes, ATB)
            x = x + r_ref[sources[s], first : first + HD, :].astype(jnp.float32) * w
        x = x.astype(jnp.bfloat16)
        rows = slice(k * HD, (k + 1) * HD)
        x_ref[rows, :] = x
        for i in range(8):
            many_ref[i, rows, :] = x


def assemble_kernel(x0_ref, x1_ref, x2_ref, x_ref, out_ref):
    b, c = spot("b"), spot("c")
    at, to = iota((HD, 2 * HD), 0), iota((HD, 2 * HD), 1)
    parts = ((x0_ref[...], b, c), (x1_ref[...], 1 - b, c), (x2_ref[0], b, 1 - c), (x2_ref[1], 1 - b, 1 - c))
    for half in range(2):
        x = jnp.zeros((NQ * HD, 2 * HD), jnp.float32)
        for part, pb, pc in parts:
            place = at - half * (HD // 2)
            col = place // GRP * HD + (pb * 2 + pc) * GRP + place % GRP
            pick = jnp.logical_and(at // (HD // 2) == half, to == col)
            x = x + dot(part, pick.astype(jnp.bfloat16))
        x_ref[half] = x.astype(jnp.bfloat16)
        mine = pl.ds(pl.multiple_of((b * 2 + c) * HD, HD), HD)
        out_ref[half * HD : (half + 1) * HD, :] = x_ref[half, mine, :]


def gram_kernel(r_ref, x_ref, h_ref):
    for i in range(8):
        part = dot(r_ref[i], x_ref[0], ATB)[0 : HD // 2] + dot(r_ref[i], x_ref[1], ATB)[HD // 2 : HD]
        h_ref[i * 2 : (i + 1) * 2] = part.astype(jnp.bfloat16).reshape(2, GRP, 2 * HD)


def call(kernel, name, outs, args, scratch=(), flops=0, moved=0, space=pltpu.VMEM, limit=40, kinds=()):
    return pl.pallas_call(
        kernel,
        out_shape=[jax.ShapeDtypeStruct(s, kind) for s, kind in zip(outs, kinds or [jnp.bfloat16] * len(outs))],
        in_specs=[pl.BlockSpec(memory_space=space)] * len(args),
        out_specs=[pl.BlockSpec(memory_space=pltpu.VMEM)] * len(outs),
        scratch_shapes=list(scratch),
        compiler_params=pltpu.CompilerParams(vmem_limit_bytes=limit << 20),
        cost_estimate=pl.CostEstimate(flops=flops, bytes_accessed=moved, transcendentals=0),
        name=name,
    )(*args)


def local(queries, keys, values):
    swap = [(0, 1), (1, 0)]
    (own,) = call(
        prep_kernel,
        "prep",
        [(NZ * NY, CUT, 2 * HD)],
        (keys, values),
        (pltpu.VMEM((2, 2, CUT, HD), jnp.bfloat16), pltpu.SemaphoreType.DMA((2, 2))),
        moved=1 << 20,
        space=pl.ANY,
        limit=60,
    )
    with jax.named_scope("q_gather"):
        near = jnp.stack([queries, lax.ppermute(queries, "xl", swap)])
        far = lax.ppermute(near, "b", swap)
    with jax.named_scope("kv_gather"):
        kv_own = lax.all_to_all(own, CHIPS, 0, 0)
        kv_own, far = lax.optimization_barrier((kv_own, far))
        kv_own = kv_own.reshape(KEYS, 2 * HD)
    with jax.named_scope("kv_swap"):
        kv_oth = lax.ppermute(kv_own, "c", swap)
    f32, bf16 = jnp.float32, jnp.bfloat16
    begun = call(
        begin_kernel,
        "attend_begin",
        [(2, ROWS, HD), (NZ, HD, TILE), (NZ, TILE, 2 * HD), (NZ, ROWS, TILE), (ROWS, HD)],
        (near, far, kv_own),
        flops=1 << 31,
        limit=24,
        kinds=(bf16, bf16, bf16, f32, f32),
    )
    (part,) = call(
        attend_kernel,
        "attend",
        [(NQ * 2, 2 * (HD + STAT), HD)],
        (*begun, kv_oth),
        (
            pltpu.VMEM((NZ, HD, TILE), bf16),
            pltpu.VMEM((NZ, TILE, 2 * HD), bf16),
            pltpu.VMEM((NC, NZ, ROWS, TILE), f32),
            pltpu.VMEM((ROWS, HD), f32),
            pltpu.VMEM((ROWS, 2 * HD), f32),
            pltpu.VMEM((ROWS, HD), f32),
            pltpu.VMEM((ROWS, HD), f32),
        ),
        flops=1 << 33,
        limit=32,
    )
    with jax.named_scope("part_exchange"):
        parts = lax.all_to_all(part, QUAD + ("xl",), 0, 0)
    x0, x_many = call(combine_kernel, "combine", [(NQ * HD, HD), (8, NQ * HD, HD)], (parts,))
    with jax.named_scope("x_swap"):
        x1 = lax.ppermute(x0, "b", swap)
        x2 = lax.ppermute(jnp.stack([x0, x1]), "c", swap)
    with jax.named_scope("x_gather"):
        x_all = lax.all_to_all(x_many, HEAD, 0, 0)
    x, attn_out = call(
        assemble_kernel,
        "assemble",
        [(2, NQ * HD, 2 * HD), (TOK, 2 * HD)],
        (x0, x1, x2),
        flops=1 << 28,
        moved=1 << 20,
    )
    (gram,) = call(gram_kernel, "gram", [(NZ * NY // 2, GRP, 2 * HD)], (x_all, x))
    with jax.named_scope("h_exchange"):
        h_parts = lax.all_to_all(gram, PAIRS, 0, 0)
    hessian = jnp.sum(h_parts.astype(jnp.float32), axis=0) * (2.0 / TOKENS)
    return attn_out, hessian


def solution(mesh):
    cut = Mesh(mesh.devices.reshape(NZ, NY // 2, 2, NC, 2, 2, 2), CTX + HEAD)
    in_specs = (P(CTX, HEAD), P(CTX, None), P(CTX, None))
    out_specs = (P(CTX, HEAD), P(CTX, HEAD))
    return jax.shard_map(local, mesh=cut, in_specs=in_specs, out_specs=out_specs, check_vma=False)
```

```python
import math

import jax
import jax.numpy as jnp
from jax import lax
from jax.experimental import pallas as pl
from jax.experimental.pallas import tpu as pltpu
from jax.sharding import Mesh
from jax.sharding import PartitionSpec as P

HEADS = 16
KVG = 2
HD = 128
TOKENS = 16384

CTX = ("zh", "yh", "b", "c")
HEAD = ("g", "xl", "zl")
CHIPS = ("yh", "b", "zh")
PAIRS = ("yh", "zh")
QUAD = ("b", "c")
SHARE = ("b", "xl")
NZ, NY, NC, NS = 4, 8, 2, 4
NQ = 4
GRP = HD // NQ
TOK = 256
CUT = TOK // NS
TILE = NY * CUT
ROWS = NS * TOK
PIECE = 256
PIECES = TILE // PIECE
SCALE = math.log2(math.e) / math.sqrt(HD)
LOW = -1e30
FLOOR = -1e29
STAT = 16
ABC = (((1,), (0,)), ((), ()))
ATB = (((0,), (0,)), ((), ()))


def dot(a, b, dims=ABC):
    return lax.dot_general(a, b, dims, preferred_element_type=jnp.float32)


def iota(shape, dim):
    return lax.broadcasted_iota(jnp.int32, shape, dim)


def spot(axes):
    return lax.axis_index(axes)


def prep_kernel(k_ref, v_ref, o_ref, kv_s, sems):
    cols = pl.ds(pl.multiple_of(spot("g") * HD, HD), HD)
    copies = []
    for b in range(2):
        rows = pl.ds(pl.multiple_of((b * 2 + spot("xl")) * CUT, CUT), CUT)
        for i, ref in enumerate((k_ref, v_ref)):
            copies.append(pltpu.make_async_copy(ref.at[rows, cols], kv_s.at[b, i], sems.at[b, i]))
    for copy in copies:
        copy.start()
    for copy in copies:
        copy.wait()
    for i in range(NZ * NY):
        for a in range(2):
            o_ref[i, :, a * HD : (a + 1) * HD] = kv_s[i // NZ % 2, a]


def lay_keys(kv_ref, k_ref, ve_ref):
    for zt in range(NZ):
        kv = kv_ref[:, zt].reshape(TILE, 2 * HD)
        k_ref[zt] = jnp.transpose(kv[:, 0:HD])
        ve_ref[zt, :, 0:HD] = kv[:, HD : 2 * HD]
        ve_ref[zt, :, HD : 2 * HD] = jnp.ones((TILE, HD), jnp.bfloat16)


def score(q, k_ref, zt, p, side, masked):
    s = dot(q, k_ref[zt, :, p * PIECE : (p + 1) * PIECE])
    if masked:
        b, c = spot("b"), spot("c")
        n = iota((ROWS, PIECE), 1) + p * PIECE
        r = iota((ROWS, PIECE), 0)
        r = r % TOK + jnp.where(r // (2 * TOK) == 0, b, 1 - b) * (NC * TOK)
        k_pos = (n // CUT) * (2 * TOK) + n % CUT + side * TOK + spot(SHARE) * CUT
        s = jnp.where(k_pos <= r + (spot("yh") * 2 * NC + c) * TOK, s, LOW)
    return s


def highest(m, s):
    for i in range(PIECE // HD):
        m = jnp.maximum(m, s[:, i * HD : (i + 1) * HD])
    return m


def begin_kernel(near_ref, far_ref, kv_ref, q_ref, k_ref, ve_ref, s0_ref, s1_ref, mx_ref):
    lay_keys(kv_ref, k_ref, ve_ref)
    for hh in range(2):
        for i in range(NS):
            part_ref = (near_ref, far_ref)[i // 2]
            q_ref[hh, i * TOK : (i + 1) * TOK, :] = part_ref[i % 2, :, hh * HD : (hh + 1) * HD]
    mx_ref[...] = jnp.full((2, ROWS, HD), LOW, jnp.float32)

    def body(zt, masked):
        for hh, s_ref, pieces in ((0, s0_ref, PIECES), (1, s1_ref, 1)):
            q = q_ref[hh]
            m = mx_ref[hh]
            for p in range(pieces):
                s = score(q, k_ref, zt, p, spot("c"), masked)
                s_ref[zt, :, p * PIECE : (p + 1) * PIECE] = s
                m = highest(m, s)
            mx_ref[hh] = m

    lax.fori_loop(0, spot("zh"), lambda zt, _: (body(zt, False), 0)[1], 0)
    body(spot("zh"), True)


def attend_kernel(
    q_ref, k0_ref, ve0_ref, s0_ref, s1_ref, mx0_ref, oth_ref, o_ref, k1_s, ve1_s, s_s, mx_s, acc_s, st_s, o0_s
):
    zh, b, c, xl = spot("zh"), spot("b"), spot("c"), spot("xl")
    lay_keys(oth_ref, k1_s, ve1_s)
    sides = ((k0_ref, ve0_ref, c), (k1_s, ve1_s, 1 - c))

    def body(zt, masked, new, old, top):
        if new is not None:
            q = q_ref[new]
            m = mx_s[...]
        if old is not None:
            acc = acc_s[...]
        for a, (k_ref, ve_ref, side) in enumerate(sides):
            for p in range(PIECES):
                at = slice(p * PIECE, (p + 1) * PIECE)
                if old is not None:
                    s_ref = s0_ref if old == 0 and a == 0 else s1_ref if old == 1 and a == 0 and p == 0 else s_s.at[a]
                    w = jnp.exp2(s_ref[zt, :, at] * SCALE - top).astype(jnp.bfloat16)
                    acc = acc + dot(w, ve_ref[zt, at, :])
                if new is not None and (a == 1 or new == 1 and p > 0):
                    s = score(q, k_ref, zt, p, side, masked)
                    s_s[a, zt, :, at] = s
                    m = highest(m, s)
        if new is not None:
            mx_s[...] = m
        if old is not None:
            acc_s[...] = acc

    def sweep(new, old, top):
        if new is not None:
            mx_s[...] = mx0_ref[new]
        if old is not None:
            acc_s[...] = jnp.zeros((ROWS, 2 * HD), jnp.float32)

        def step(zt, _):
            body(zt, False, new, old, top)
            return 0

        lax.fori_loop(0, zh, step, 0)
        body(zh, True, new, old, top)

    def tops():
        return jnp.maximum(jnp.max(mx_s[...], axis=1, keepdims=True), FLOOR) * SCALE

    def finish(hh, top):
        total = acc_s[:, HD : 2 * HD]
        some = total > 0.0
        safe = jnp.where(some, total, 1.0)
        lse = jnp.where(some, top + jnp.log2(safe), LOW)
        hi = lse.astype(jnp.bfloat16).astype(jnp.float32)
        mid = (lse - hi).astype(jnp.bfloat16).astype(jnp.float32)
        lane = iota((ROWS, HD), 1) - 3 * hh
        parts = jnp.where(lane == 0, hi, jnp.where(lane == 1, mid, lse - hi - mid))
        return acc_s[:, 0:HD] / safe, parts

    sweep(0, None, None)
    top0 = tops()
    sweep(1, 0, top0)
    o0_s[...], st_s[...] = finish(0, top0)
    top1 = tops()
    sweep(None, 1, top1)
    o1, st1 = finish(1, top1)
    stats = jnp.where(iota((ROWS, HD), 1) < 3, st_s[...], st1)
    place = iota((TOK // 2, HD), 1) // GRP

    def swap(a, b, by):
        even = place // (by // GRP) % 2 == 0
        return (
            jnp.where(even, a, pltpu.roll(b, by, 1)),
            jnp.where(even, pltpu.roll(a, HD - by, 1), b),
        )

    for i in range(NS):
        to_x = xl + (1 - 2 * xl) * (i % 2)
        to_b = b + (1 - 2 * b) * (i // 2)
        rows = pl.ds(pl.multiple_of(to_b * HD, HD), HD)
        tails = pl.ds(pl.multiple_of(2 * HD + to_b * STAT, STAT), STAT)
        at = i * TOK
        mid, end = at + TOK // 2, at + TOK
        low0, low1 = swap(o0_s[at:mid], o1[at:mid], GRP)
        high0, high1 = swap(o0_s[mid:end], o1[mid:end], GRP)
        slots = [None] * NQ
        slots[0], slots[2] = swap(low0, high0, 2 * GRP)
        slots[1], slots[3] = swap(low1, high1, 2 * GRP)
        turned = jnp.transpose(stats[at:end])
        tail = jnp.concatenate([turned[0:8, 0:HD], turned[0:8, HD : 2 * HD]], axis=0)
        for k in range(NQ):
            o_ref[to_x * NQ + k, rows, :] = slots[k].astype(jnp.bfloat16)
            o_ref[to_x * NQ + k, tails, :] = tail.astype(jnp.bfloat16)


def combine_kernel(r_ref, x_ref, many_ref):
    row = iota((STAT, HD), 0)
    lanes = jnp.logical_and(row % NQ == iota((STAT, HD), 1) // GRP, row < 3 * NQ).astype(jnp.bfloat16)
    for k in range(NQ):
        sources = [s % 2 * NQ + s // 2 * NC + k % NC for s in range(NS)]
        first, stat = k // NC * HD, 2 * HD + k // NC * STAT
        shares = [[] for _ in range(NS)]
        for place in range(NQ):
            lses = []
            for s in sources:
                at = place // 2 * 8 + place % 2 * 3
                t = r_ref[s, stat : stat + STAT, :].astype(jnp.float32)[at : at + 3]
                lses.append(t[0:1] + t[1:2] + t[2:3])
            top = jnp.maximum(jnp.maximum(lses[0], lses[1]), jnp.maximum(lses[2], lses[3]))
            w = [jnp.exp2(lse - top) for lse in lses]
            inv = 1.0 / (w[0] + w[1] + w[2] + w[3])
            for s in range(NS):
                shares[s].append(w[s] * inv)
        x = jnp.zeros((HD, HD), jnp.float32)
        for s in range(NS):
            w = jnp.concatenate(shares[s], axis=0)
            hi = w.astype(jnp.bfloat16).astype(jnp.float32)
            mid = (w - hi).astype(jnp.bfloat16).astype(jnp.float32)
            lever = jnp.concatenate([hi, mid, w - hi - mid, jnp.zeros_like(w)], axis=0)
            w = dot(lever.astype(jnp.bfloat16), lanes, ATB)
            x = x + r_ref[sources[s], first : first + HD, :].astype(jnp.float32) * w
        x = x.astype(jnp.bfloat16)
        rows = slice(k * HD, (k + 1) * HD)
        x_ref[rows, :] = x
        for i in range(8):
            many_ref[i, rows, :] = x


def assemble_kernel(x0_ref, x1_ref, x2_ref, x_ref, out_ref):
    b, c = spot("b"), spot("c")
    at, to = iota((HD, 2 * HD), 0), iota((HD, 2 * HD), 1)
    parts = ((x0_ref[...], b, c), (x1_ref[...], 1 - b, c), (x2_ref[0], b, 1 - c), (x2_ref[1], 1 - b, 1 - c))
    for half in range(2):
        x = jnp.zeros((NQ * HD, 2 * HD), jnp.float32)
        for part, pb, pc in parts:
            place = at - half * (HD // 2)
            col = place // GRP * HD + (pb * 2 + pc) * GRP + place % GRP
            pick = jnp.logical_and(at // (HD // 2) == half, to == col)
            x = x + dot(part, pick.astype(jnp.bfloat16))
        x_ref[half] = x.astype(jnp.bfloat16)
        mine = pl.ds(pl.multiple_of((b * 2 + c) * HD, HD), HD)
        out_ref[half * HD : (half + 1) * HD, :] = x_ref[half, mine, :]


def gram_kernel(r_ref, x_ref, h_ref):
    for i in range(8):
        at = i % 2 * 4 + i // 2
        part = dot(r_ref[at], x_ref[0], ATB)[0 : HD // 2] + dot(r_ref[at], x_ref[1], ATB)[HD // 2 : HD]
        for hh in range(2):
            zh, yh = (i * 2 + hh) // 4, (i * 2 + hh) % 4
            h_ref[yh * NZ + zh] = part[hh * GRP : (hh + 1) * GRP].astype(jnp.bfloat16)


def call(kernel, name, outs, args, scratch=(), flops=0, moved=0, space=pltpu.VMEM, limit=40, kinds=()):
    return pl.pallas_call(
        kernel,
        out_shape=[jax.ShapeDtypeStruct(s, kind) for s, kind in zip(outs, kinds or [jnp.bfloat16] * len(outs))],
        in_specs=[pl.BlockSpec(memory_space=space)] * len(args),
        out_specs=[pl.BlockSpec(memory_space=pltpu.VMEM)] * len(outs),
        scratch_shapes=list(scratch),
        compiler_params=pltpu.CompilerParams(vmem_limit_bytes=limit << 20),
        cost_estimate=pl.CostEstimate(flops=flops, bytes_accessed=moved, transcendentals=0),
        name=name,
    )(*args)


def local(queries, keys, values):
    swap = [(0, 1), (1, 0)]
    (own,) = call(
        prep_kernel,
        "prep",
        [(NZ * NY, CUT, 2 * HD)],
        (keys, values),
        (pltpu.VMEM((2, 2, CUT, HD), jnp.bfloat16), pltpu.SemaphoreType.DMA((2, 2))),
        moved=1 << 20,
        space=pl.ANY,
        limit=60,
    )
    with jax.named_scope("q_gather"):
        near = jnp.stack([queries, lax.ppermute(queries, "xl", swap)])
        far = lax.ppermute(near, "b", swap)
    with jax.named_scope("kv_gather"):
        kv_own = lax.all_to_all(own, CHIPS, 0, 0)
        kv_own, far = lax.optimization_barrier((kv_own, far))
        kv_own = kv_own.reshape(NY, NZ, CUT, 2 * HD)
    with jax.named_scope("kv_swap"):
        kv_oth = lax.ppermute(kv_own, "c", swap)
    f32, bf16 = jnp.float32, jnp.bfloat16
    begun = call(
        begin_kernel,
        "attend_begin",
        [(2, ROWS, HD), (NZ, HD, TILE), (NZ, TILE, 2 * HD), (NZ, ROWS, TILE), (NZ, ROWS, PIECE), (2, ROWS, HD)],
        (near, far, kv_own),
        flops=1 << 31,
        limit=16,
        kinds=(bf16, bf16, bf16, f32, f32, f32),
    )
    (part,) = call(
        attend_kernel,
        "attend",
        [(NQ * 2, 2 * (HD + STAT), HD)],
        (*begun, kv_oth),
        (
            pltpu.VMEM((NZ, HD, TILE), bf16),
            pltpu.VMEM((NZ, TILE, 2 * HD), bf16),
            pltpu.VMEM((NC, NZ, ROWS, TILE), f32),
            pltpu.VMEM((ROWS, HD), f32),
            pltpu.VMEM((ROWS, 2 * HD), f32),
            pltpu.VMEM((ROWS, HD), f32),
            pltpu.VMEM((ROWS, HD), f32),
        ),
        flops=1 << 33,
        limit=28,
    )
    with jax.named_scope("part_exchange"):
        parts = lax.all_to_all(part, ("xl",) + QUAD, 0, 0)
    x0, x_many = call(combine_kernel, "combine", [(NQ * HD, HD), (8, NQ * HD, HD)], (parts,))
    with jax.named_scope("x_swap"):
        x1 = lax.ppermute(x0, "b", swap)
        x2 = lax.ppermute(jnp.stack([x0, x1]), "c", swap)
    with jax.named_scope("x_gather"):
        x_all = lax.all_to_all(x_many, ("zl", "g", "xl"), 0, 0)
    x, attn_out = call(
        assemble_kernel,
        "assemble",
        [(2, NQ * HD, 2 * HD), (TOK, 2 * HD)],
        (x0, x1, x2),
        flops=1 << 28,
        moved=1 << 20,
    )
    (gram,) = call(gram_kernel, "gram", [(NZ * NY // 2, GRP, 2 * HD)], (x_all, x))
    with jax.named_scope("h_exchange"):
        h_parts = lax.all_to_all(gram, PAIRS, 0, 0)
    hessian = jnp.sum(h_parts.astype(jnp.float32), axis=0) * (2.0 / TOKENS)
    return attn_out, hessian


def solution(mesh):
    cut = Mesh(mesh.devices.reshape(NZ, NY // 2, 2, NC, 2, 2, 2), CTX + HEAD)
    in_specs = (P(CTX, HEAD), P(CTX, None), P(CTX, None))
    out_specs = (P(CTX, HEAD), P(CTX, HEAD))
    return jax.shard_map(local, mesh=cut, in_specs=in_specs, out_specs=out_specs, check_vma=False)
```

```python
import math

import jax
import jax.numpy as jnp
from jax import lax
from jax.experimental import pallas as pl
from jax.experimental.pallas import tpu as pltpu
from jax.sharding import Mesh
from jax.sharding import PartitionSpec as P

HEADS = 16
KVG = 2
HD = 128
TOKENS = 16384

CTX = ("zh", "yh", "b", "c")
HEAD = ("g", "xl", "zl")
CHIPS = ("yh", "b", "zh")
PAIRS = ("yh", "zh")
QUAD = ("b", "c")
SHARE = ("b", "xl")
NZ, NY, NC, NS = 4, 8, 2, 4
NQ = 4
GRP = HD // NQ
TOK = 256
CUT = TOK // NS
TILE = NY * CUT
ROWS = NS * TOK
PIECE = 256
PIECES = TILE // PIECE
SCALE = math.log2(math.e) / math.sqrt(HD)
LOW = -1e30
FLOOR = -1e29
STAT = 16
ABC = (((1,), (0,)), ((), ()))
ATB = (((0,), (0,)), ((), ()))


def dot(a, b, dims=ABC):
    return lax.dot_general(a, b, dims, preferred_element_type=jnp.float32)


def iota(shape, dim):
    return lax.broadcasted_iota(jnp.int32, shape, dim)


def spot(axes):
    return lax.axis_index(axes)


def prep_kernel(k_ref, v_ref, o_ref, kv_s, sems):
    cols = pl.ds(pl.multiple_of(spot("g") * HD, HD), HD)
    copies = []
    for b in range(2):
        rows = pl.ds(pl.multiple_of((b * 2 + spot("xl")) * CUT, CUT), CUT)
        for i, ref in enumerate((k_ref, v_ref)):
            copies.append(pltpu.make_async_copy(ref.at[rows, cols], kv_s.at[b, i], sems.at[b, i]))
    for copy in copies:
        copy.start()
    for copy in copies:
        copy.wait()
    for i in range(NZ * NY):
        for a in range(2):
            o_ref[i, :, a * HD : (a + 1) * HD] = kv_s[i // NZ % 2, a]


def lay_keys(kv_ref, k_ref, ve_ref):
    for zt in range(NZ):
        kv = kv_ref[:, zt].reshape(TILE, 2 * HD)
        k_ref[zt] = jnp.transpose(kv[:, 0:HD])
        ve_ref[zt, :, 0:HD] = kv[:, HD : 2 * HD]
        ve_ref[zt, :, HD : 2 * HD] = jnp.ones((TILE, HD), jnp.bfloat16)


def score(q, k_ref, zt, p, side, masked):
    s = dot(q, k_ref[zt, :, p * PIECE : (p + 1) * PIECE])
    if masked:
        b, c = spot("b"), spot("c")
        n = iota((ROWS, PIECE), 1) + p * PIECE
        r = iota((ROWS, PIECE), 0)
        r = r % TOK + jnp.where(r // (2 * TOK) == 0, b, 1 - b) * (NC * TOK)
        k_pos = (n // CUT) * (2 * TOK) + n % CUT + side * TOK + spot(SHARE) * CUT
        s = jnp.where(k_pos <= r + (spot("yh") * 2 * NC + c) * TOK, s, LOW)
    return s


def highest(m, s):
    for i in range(PIECE // HD):
        m = jnp.maximum(m, s[:, i * HD : (i + 1) * HD])
    return m


def begin_kernel(near_ref, far_ref, kv_ref, q_ref, k_ref, ve_ref, s0_ref, s1_ref, mx_ref):
    lay_keys(kv_ref, k_ref, ve_ref)
    for hh in range(2):
        for i in range(NS):
            part_ref = (near_ref, far_ref)[i // 2]
            q_ref[hh, i * TOK : (i + 1) * TOK, :] = part_ref[i % 2, :, hh * HD : (hh + 1) * HD]
    mx_ref[...] = jnp.full((2, ROWS, HD), LOW, jnp.float32)

    def body(zt, masked):
        for hh, s_ref, pieces in ((0, s0_ref, PIECES), (1, s1_ref, 1)):
            q = q_ref[hh]
            m = mx_ref[hh]
            for p in range(pieces):
                s = score(q, k_ref, zt, p, spot("c"), masked)
                s_ref[zt, :, p * PIECE : (p + 1) * PIECE] = s
                m = highest(m, s)
            mx_ref[hh] = m

    lax.fori_loop(0, spot("zh"), lambda zt, _: (body(zt, False), 0)[1], 0)
    body(spot("zh"), True)


def attend_kernel(
    q_ref, k0_ref, ve0_ref, s0_ref, s1_ref, mx0_ref, oth_ref, o_ref, k1_s, ve1_s, s_s, mx_s, acc_s, st_s, o0_s
):
    zh, b, c, xl = spot("zh"), spot("b"), spot("c"), spot("xl")
    lay_keys(oth_ref, k1_s, ve1_s)
    sides = ((k0_ref, ve0_ref, c), (k1_s, ve1_s, 1 - c))

    def body(zt, masked, new, old, top):
        if new is not None:
            q = q_ref[new]
            m = mx_s[...]
        if old is not None:
            acc = acc_s[...]
        for a, (k_ref, ve_ref, side) in enumerate(sides):
            for p in range(PIECES):
                at = slice(p * PIECE, (p + 1) * PIECE)
                if old is not None:
                    s_ref = s0_ref if old == 0 and a == 0 else s1_ref if old == 1 and a == 0 and p == 0 else s_s.at[a]
                    w = jnp.exp2(s_ref[zt, :, at] * SCALE - top).astype(jnp.bfloat16)
                    acc = acc + dot(w, ve_ref[zt, at, :])
                if new is not None and (a == 1 or new == 1 and p > 0):
                    s = score(q, k_ref, zt, p, side, masked)
                    s_s[a, zt, :, at] = s
                    m = highest(m, s)
        if new is not None:
            mx_s[...] = m
        if old is not None:
            acc_s[...] = acc

    def sweep(new, old, top):
        if new is not None:
            mx_s[...] = mx0_ref[new]
        if old is not None:
            acc_s[...] = jnp.zeros((ROWS, 2 * HD), jnp.float32)

        def step(zt, _):
            body(zt, False, new, old, top)
            return 0

        lax.fori_loop(0, zh, step, 0)
        body(zh, True, new, old, top)

    def tops():
        return jnp.maximum(jnp.max(mx_s[...], axis=1, keepdims=True), FLOOR) * SCALE

    def finish(hh, top):
        total = acc_s[:, HD : 2 * HD]
        some = total > 0.0
        safe = jnp.where(some, total, 1.0)
        lse = jnp.where(some, top + jnp.log2(safe), LOW)
        hi = lse.astype(jnp.bfloat16).astype(jnp.float32)
        mid = (lse - hi).astype(jnp.bfloat16).astype(jnp.float32)
        lane = iota((ROWS, HD), 1) - 3 * hh
        parts = jnp.where(lane == 0, hi, jnp.where(lane == 1, mid, lse - hi - mid))
        return acc_s[:, 0:HD] / safe, parts

    sweep(0, None, None)
    top0 = tops()
    sweep(1, 0, top0)
    o0_s[...], st_s[...] = finish(0, top0)
    top1 = tops()
    sweep(None, 1, top1)
    o1, st1 = finish(1, top1)
    stats = jnp.where(iota((ROWS, HD), 1) < 3, st_s[...], st1)
    place = iota((TOK // 2, HD), 1) // GRP

    def swap(a, b, by):
        even = place // (by // GRP) % 2 == 0
        return (
            jnp.where(even, a, pltpu.roll(b, by, 1)),
            jnp.where(even, pltpu.roll(a, HD - by, 1), b),
        )

    for i in range(NS):
        to_x = xl + (1 - 2 * xl) * (i % 2)
        to_b = b + (1 - 2 * b) * (i // 2)
        rows = pl.ds(pl.multiple_of(to_b * HD, HD), HD)
        tails = pl.ds(pl.multiple_of(2 * HD + to_b * STAT, STAT), STAT)
        at = i * TOK
        mid, end = at + TOK // 2, at + TOK
        low0, low1 = swap(o0_s[at:mid], o1[at:mid], GRP)
        high0, high1 = swap(o0_s[mid:end], o1[mid:end], GRP)
        slots = [None] * NQ
        slots[0], slots[2] = swap(low0, high0, 2 * GRP)
        slots[1], slots[3] = swap(low1, high1, 2 * GRP)
        turned = jnp.transpose(stats[at:end])
        tail = jnp.concatenate([turned[0:8, 0:HD], turned[0:8, HD : 2 * HD]], axis=0)
        for k in range(NQ):
            o_ref[to_x * NQ + k, rows, :] = slots[k].astype(jnp.bfloat16)
            o_ref[to_x * NQ + k, tails, :] = tail.astype(jnp.bfloat16)


def combine_kernel(r_ref, x_ref, many_ref):
    row = iota((STAT, HD), 0)
    lanes = jnp.logical_and(row % NQ == iota((STAT, HD), 1) // GRP, row < 3 * NQ).astype(jnp.bfloat16)
    for k in range(NQ):
        sources = [s % 2 * NQ + s // 2 * NC + k % NC for s in range(NS)]
        first, stat = k // NC * HD, 2 * HD + k // NC * STAT
        shares = [[] for _ in range(NS)]
        for place in range(NQ):
            lses = []
            for s in sources:
                at = place // 2 * 8 + place % 2 * 3
                t = r_ref[s, stat : stat + STAT, :].astype(jnp.float32)[at : at + 3]
                lses.append(t[0:1] + t[1:2] + t[2:3])
            top = jnp.maximum(jnp.maximum(lses[0], lses[1]), jnp.maximum(lses[2], lses[3]))
            w = [jnp.exp2(lse - top) for lse in lses]
            inv = 1.0 / (w[0] + w[1] + w[2] + w[3])
            for s in range(NS):
                shares[s].append(w[s] * inv)
        x = jnp.zeros((HD, HD), jnp.float32)
        for s in range(NS):
            w = jnp.concatenate(shares[s], axis=0)
            hi = w.astype(jnp.bfloat16).astype(jnp.float32)
            mid = (w - hi).astype(jnp.bfloat16).astype(jnp.float32)
            lever = jnp.concatenate([hi, mid, w - hi - mid, jnp.zeros_like(w)], axis=0)
            w = dot(lever.astype(jnp.bfloat16), lanes, ATB)
            x = x + r_ref[sources[s], first : first + HD, :].astype(jnp.float32) * w
        x = x.astype(jnp.bfloat16)
        rows = slice(k * HD, (k + 1) * HD)
        x_ref[rows, :] = x
        for i in range(8):
            many_ref[i, rows, :] = x


def assemble_kernel(x0_ref, x1_ref, x2_ref, x_ref, out_ref):
    b, c = spot("b"), spot("c")
    at, to = iota((HD, 2 * HD), 0), iota((HD, 2 * HD), 1)
    parts = ((x0_ref[...], b, c), (x1_ref[...], 1 - b, c), (x2_ref[0], b, 1 - c), (x2_ref[1], 1 - b, 1 - c))
    for half in range(2):
        x = jnp.zeros((NQ * HD, 2 * HD), jnp.float32)
        for part, pb, pc in parts:
            place = at - half * (HD // 2)
            col = place // GRP * HD + (pb * 2 + pc) * GRP + place % GRP
            pick = jnp.logical_and(at // (HD // 2) == half, to == col)
            x = x + dot(part, pick.astype(jnp.bfloat16))
        x_ref[half] = x.astype(jnp.bfloat16)
        mine = pl.ds(pl.multiple_of((b * 2 + c) * HD, HD), HD)
        out_ref[half * HD : (half + 1) * HD, :] = x_ref[half, mine, :]


def gram_kernel(r_ref, x_ref, h_ref):
    for i in range(8):
        at = i % 2 * 4 + i // 2
        part = dot(r_ref[at], x_ref[0], ATB)[0 : HD // 2] + dot(r_ref[at], x_ref[1], ATB)[HD // 2 : HD]
        for hh in range(2):
            zh, yh = (i * 2 + hh) // 4, (i * 2 + hh) % 4
            h_ref[yh * NZ + zh] = (part[hh * GRP : (hh + 1) * GRP] * (2.0 / TOKENS)).astype(jnp.bfloat16)


def call(kernel, name, outs, args, scratch=(), flops=0, moved=0, space=pltpu.VMEM, limit=40, kinds=()):
    return pl.pallas_call(
        kernel,
        out_shape=[jax.ShapeDtypeStruct(s, kind) for s, kind in zip(outs, kinds or [jnp.bfloat16] * len(outs))],
        in_specs=[pl.BlockSpec(memory_space=space)] * len(args),
        out_specs=[pl.BlockSpec(memory_space=pltpu.VMEM)] * len(outs),
        scratch_shapes=list(scratch),
        compiler_params=pltpu.CompilerParams(vmem_limit_bytes=limit << 20),
        cost_estimate=pl.CostEstimate(flops=flops, bytes_accessed=moved, transcendentals=0),
        name=name,
    )(*args)


def local(queries, keys, values):
    swap = [(0, 1), (1, 0)]
    (own,) = call(
        prep_kernel,
        "prep",
        [(NZ * NY, CUT, 2 * HD)],
        (keys, values),
        (pltpu.VMEM((2, 2, CUT, HD), jnp.bfloat16), pltpu.SemaphoreType.DMA((2, 2))),
        moved=1 << 20,
        space=pl.ANY,
        limit=60,
    )
    with jax.named_scope("q_gather"):
        near = jnp.stack([queries, lax.ppermute(queries, "xl", swap)])
        far = lax.ppermute(near, "b", swap)
    with jax.named_scope("kv_gather"):
        kv_own = lax.all_to_all(own, CHIPS, 0, 0)
        kv_own, far = lax.optimization_barrier((kv_own, far))
        kv_own = kv_own.reshape(NY, NZ, CUT, 2 * HD)
    with jax.named_scope("kv_swap"):
        kv_oth = lax.ppermute(kv_own, "c", swap)
    f32, bf16 = jnp.float32, jnp.bfloat16
    begun = call(
        begin_kernel,
        "attend_begin",
        [(2, ROWS, HD), (NZ, HD, TILE), (NZ, TILE, 2 * HD), (NZ, ROWS, TILE), (NZ, ROWS, PIECE), (2, ROWS, HD)],
        (near, far, kv_own),
        flops=1 << 31,
        limit=16,
        kinds=(bf16, bf16, bf16, f32, f32, f32),
    )
    (part,) = call(
        attend_kernel,
        "attend",
        [(NQ * 2, 2 * (HD + STAT), HD)],
        (*begun, kv_oth),
        (
            pltpu.VMEM((NZ, HD, TILE), bf16),
            pltpu.VMEM((NZ, TILE, 2 * HD), bf16),
            pltpu.VMEM((NC, NZ, ROWS, TILE), f32),
            pltpu.VMEM((ROWS, HD), f32),
            pltpu.VMEM((ROWS, 2 * HD), f32),
            pltpu.VMEM((ROWS, HD), f32),
            pltpu.VMEM((ROWS, HD), f32),
        ),
        flops=1 << 33,
        limit=28,
    )
    with jax.named_scope("part_exchange"):
        parts = lax.all_to_all(part, ("xl",) + QUAD, 0, 0)
    x0, x_many = call(combine_kernel, "combine", [(NQ * HD, HD), (8, NQ * HD, HD)], (parts,))
    with jax.named_scope("x_swap"):
        x1 = lax.ppermute(x0, "b", swap)
        x2 = lax.ppermute(jnp.stack([x0, x1]), "c", swap)
    with jax.named_scope("x_gather"):
        x_all = lax.all_to_all(x_many, ("zl", "g", "xl"), 0, 0)
    x, attn_out = call(
        assemble_kernel,
        "assemble",
        [(2, NQ * HD, 2 * HD), (TOK, 2 * HD)],
        (x0, x1, x2),
        flops=1 << 28,
        moved=1 << 20,
    )
    (gram,) = call(gram_kernel, "gram", [(NZ * NY // 2, GRP, 2 * HD)], (x_all, x))
    with jax.named_scope("h_exchange"):
        h_parts = lax.all_to_all(gram, PAIRS, 0, 0)
    hessian = jnp.sum(h_parts.astype(jnp.float32), axis=0)
    return attn_out, hessian


def solution(mesh):
    cut = Mesh(mesh.devices.reshape(NZ, NY // 2, 2, NC, 2, 2, 2), CTX + HEAD)
    in_specs = (P(CTX, HEAD), P(CTX, None), P(CTX, None))
    out_specs = (P(CTX, HEAD), P(CTX, HEAD))
    return jax.shard_map(local, mesh=cut, in_specs=in_specs, out_specs=out_specs, check_vma=False)
```

```python
import math

import jax
import jax.numpy as jnp
from jax import lax
from jax.experimental import pallas as pl
from jax.experimental.pallas import tpu as pltpu
from jax.sharding import Mesh
from jax.sharding import PartitionSpec as P

HEADS = 16
KVG = 2
HD = 128
TOKENS = 16384

CTX = ("zh", "yh", "b", "c")
HEAD = ("g", "xl", "zl")
CHIPS = ("yh", "b", "zh")
PAIRS = ("yh", "zh")
QUAD = ("b", "c")
SHARE = ("b", "xl")
NZ, NY, NC, NS = 4, 8, 2, 4
NQ = 4
GRP = HD // NQ
TOK = 256
CUT = TOK // NS
TILE = NY * CUT
ROWS = NS * TOK
PIECE = 256
PIECES = TILE // PIECE
SCALE = math.log2(math.e) / math.sqrt(HD)
LOW = -1e30
FLOOR = -1e29
STAT = 16
ABC = (((1,), (0,)), ((), ()))
ATB = (((0,), (0,)), ((), ()))


def dot(a, b, dims=ABC):
    return lax.dot_general(a, b, dims, preferred_element_type=jnp.float32)


def iota(shape, dim):
    return lax.broadcasted_iota(jnp.int32, shape, dim)


def spot(axes):
    return lax.axis_index(axes)


def prep_kernel(k_ref, v_ref, o_ref, kv_s, sems):
    cols = pl.ds(pl.multiple_of(spot("g") * HD, HD), HD)
    copies = []
    for b in range(2):
        rows = pl.ds(pl.multiple_of((b * 2 + spot("xl")) * CUT, CUT), CUT)
        for i, ref in enumerate((k_ref, v_ref)):
            copies.append(pltpu.make_async_copy(ref.at[rows, cols], kv_s.at[b, i], sems.at[b, i]))
    for copy in copies:
        copy.start()
    for copy in copies:
        copy.wait()
    for i in range(NZ * NY):
        for a in range(2):
            o_ref[i, :, a * HD : (a + 1) * HD] = kv_s[i // NZ % 2, a]


def lay_keys(kv_ref, k_ref, ve_ref):
    for zt in range(NZ):
        kv = kv_ref[:, zt].reshape(TILE, 2 * HD)
        k_ref[zt] = jnp.transpose(kv[:, 0:HD])
        ve_ref[zt, :, 0:HD] = kv[:, HD : 2 * HD]
        ve_ref[zt, :, HD : 2 * HD] = jnp.ones((TILE, HD), jnp.bfloat16)


def score(q, k_ref, zt, p, side, masked):
    s = dot(q, k_ref[zt, :, p * PIECE : (p + 1) * PIECE])
    if masked:
        b, c = spot("b"), spot("c")
        n = iota((ROWS, PIECE), 1) + p * PIECE
        r = iota((ROWS, PIECE), 0)
        r = r % TOK + jnp.where(r // (2 * TOK) == 0, b, 1 - b) * (NC * TOK)
        k_pos = (n // CUT) * (2 * TOK) + n % CUT + side * TOK + spot(SHARE) * CUT
        s = jnp.where(k_pos <= r + (spot("yh") * 2 * NC + c) * TOK, s, LOW)
    return s


def highest(m, s):
    for i in range(PIECE // HD):
        m = jnp.maximum(m, s[:, i * HD : (i + 1) * HD])
    return m


def begin_kernel(near_ref, far_ref, kv_ref, q_ref, k_ref, ve_ref, s0_ref, s1_ref, mx_ref):
    lay_keys(kv_ref, k_ref, ve_ref)
    for hh in range(2):
        for i in range(NS):
            part_ref = (near_ref, far_ref)[i // 2]
            q_ref[hh, i * TOK : (i + 1) * TOK, :] = part_ref[i % 2, :, hh * HD : (hh + 1) * HD]
    mx_ref[...] = jnp.full((2, ROWS, HD), LOW, jnp.float32)

    def body(zt, masked):
        for hh, s_ref, pieces in ((0, s0_ref, PIECES), (1, s1_ref, 1)):
            q = q_ref[hh]
            m = mx_ref[hh]
            for p in range(pieces):
                s = score(q, k_ref, zt, p, spot("c"), masked)
                s_ref[zt, :, p * PIECE : (p + 1) * PIECE] = s
                m = highest(m, s)
            mx_ref[hh] = m

    lax.fori_loop(0, spot("zh"), lambda zt, _: (body(zt, False), 0)[1], 0)
    body(spot("zh"), True)


def attend_kernel(
    q_ref, k0_ref, ve0_ref, s0_ref, s1_ref, mx0_ref, oth_ref, o_ref, k1_s, ve1_s, s_s, mx_s, acc_s, st_s, o0_s
):
    zh, b, c, xl = spot("zh"), spot("b"), spot("c"), spot("xl")
    lay_keys(oth_ref, k1_s, ve1_s)
    sides = ((k0_ref, ve0_ref, c), (k1_s, ve1_s, 1 - c))

    def body(zt, masked, new, old, top):
        if new is not None:
            q = q_ref[new]
            m = mx_s[...]
        if old is not None:
            acc = acc_s[...]
        for a, (k_ref, ve_ref, side) in enumerate(sides):
            for p in range(PIECES):
                at = slice(p * PIECE, (p + 1) * PIECE)
                if old is not None:
                    s_ref = s0_ref if old == 0 and a == 0 else s1_ref if old == 1 and a == 0 and p == 0 else s_s.at[a]
                    w = jnp.exp2(s_ref[zt, :, at] * SCALE - top).astype(jnp.bfloat16)
                    acc = acc + dot(w, ve_ref[zt, at, :])
                if new is not None and (a == 1 or new == 1 and p > 0):
                    s = score(q, k_ref, zt, p, side, masked)
                    s_s[a, zt, :, at] = s
                    m = highest(m, s)
        if new is not None:
            mx_s[...] = m
        if old is not None:
            acc_s[...] = acc

    def sweep(new, old, top):
        if new is not None:
            mx_s[...] = mx0_ref[new]
        if old is not None:
            acc_s[...] = jnp.zeros((ROWS, 2 * HD), jnp.float32)

        def step(zt, _):
            body(zt, False, new, old, top)
            return 0

        lax.fori_loop(0, zh + (new is None), step, 0)
        if new is not None:
            body(zh, True, new, old, top)

    def tops():
        return jnp.maximum(jnp.max(mx_s[...], axis=1, keepdims=True), FLOOR) * SCALE

    def finish(hh, top):
        total = acc_s[:, HD : 2 * HD]
        some = total > 0.0
        safe = jnp.where(some, total, 1.0)
        lse = jnp.where(some, top + jnp.log2(safe), LOW)
        hi = lse.astype(jnp.bfloat16).astype(jnp.float32)
        mid = (lse - hi).astype(jnp.bfloat16).astype(jnp.float32)
        lane = iota((ROWS, HD), 1) - 3 * hh
        parts = jnp.where(lane == 0, hi, jnp.where(lane == 1, mid, lse - hi - mid))
        return acc_s[:, 0:HD] / safe, parts

    sweep(0, None, None)
    top0 = tops()
    sweep(1, 0, top0)
    o0_s[...], st_s[...] = finish(0, top0)
    top1 = tops()
    sweep(None, 1, top1)
    o1, st1 = finish(1, top1)
    stats = jnp.where(iota((ROWS, HD), 1) < 3, st_s[...], st1)
    place = iota((TOK // 2, HD), 1) // GRP

    def swap(a, b, by):
        even = place // (by // GRP) % 2 == 0
        return (
            jnp.where(even, a, pltpu.roll(b, by, 1)),
            jnp.where(even, pltpu.roll(a, HD - by, 1), b),
        )

    for i in range(NS):
        to_x = xl + (1 - 2 * xl) * (i % 2)
        to_b = b + (1 - 2 * b) * (i // 2)
        rows = pl.ds(pl.multiple_of(to_b * HD, HD), HD)
        tails = pl.ds(pl.multiple_of(2 * HD + to_b * STAT, STAT), STAT)
        at = i * TOK
        mid, end = at + TOK // 2, at + TOK
        low0, low1 = swap(o0_s[at:mid], o1[at:mid], GRP)
        high0, high1 = swap(o0_s[mid:end], o1[mid:end], GRP)
        slots = [None] * NQ
        slots[0], slots[2] = swap(low0, high0, 2 * GRP)
        slots[1], slots[3] = swap(low1, high1, 2 * GRP)
        turned = jnp.transpose(stats[at:end])
        tail = jnp.concatenate([turned[0:8, 0:HD], turned[0:8, HD : 2 * HD]], axis=0)
        for k in range(NQ):
            o_ref[to_x * NQ + k, rows, :] = slots[k].astype(jnp.bfloat16)
            o_ref[to_x * NQ + k, tails, :] = tail.astype(jnp.bfloat16)


def combine_kernel(r_ref, x_ref, many_ref):
    row = iota((STAT, HD), 0)
    lanes = jnp.logical_and(row % NQ == iota((STAT, HD), 1) // GRP, row < 3 * NQ).astype(jnp.bfloat16)
    for k in range(NQ):
        sources = [s % 2 * NQ + s // 2 * NC + k % NC for s in range(NS)]
        first, stat = k // NC * HD, 2 * HD + k // NC * STAT
        shares = [[] for _ in range(NS)]
        for place in range(NQ):
            lses = []
            for s in sources:
                at = place // 2 * 8 + place % 2 * 3
                t = r_ref[s, stat : stat + STAT, :].astype(jnp.float32)[at : at + 3]
                lses.append(t[0:1] + t[1:2] + t[2:3])
            top = jnp.maximum(jnp.maximum(lses[0], lses[1]), jnp.maximum(lses[2], lses[3]))
            w = [jnp.exp2(lse - top) for lse in lses]
            inv = 1.0 / (w[0] + w[1] + w[2] + w[3])
            for s in range(NS):
                shares[s].append(w[s] * inv)
        x = jnp.zeros((HD, HD), jnp.float32)
        for s in range(NS):
            w = jnp.concatenate(shares[s], axis=0)
            hi = w.astype(jnp.bfloat16).astype(jnp.float32)
            mid = (w - hi).astype(jnp.bfloat16).astype(jnp.float32)
            lever = jnp.concatenate([hi, mid, w - hi - mid, jnp.zeros_like(w)], axis=0)
            w = dot(lever.astype(jnp.bfloat16), lanes, ATB)
            x = x + r_ref[sources[s], first : first + HD, :].astype(jnp.float32) * w
        x = x.astype(jnp.bfloat16)
        rows = slice(k * HD, (k + 1) * HD)
        x_ref[rows, :] = x
        for i in range(8):
            many_ref[i, rows, :] = x


def assemble_kernel(x0_ref, x1_ref, x2_ref, x_ref, out_ref):
    b, c = spot("b"), spot("c")
    at, to = iota((HD, 2 * HD), 0), iota((HD, 2 * HD), 1)
    parts = ((x0_ref[...], b, c), (x1_ref[...], 1 - b, c), (x2_ref[0], b, 1 - c), (x2_ref[1], 1 - b, 1 - c))
    for half in range(2):
        x = jnp.zeros((NQ * HD, 2 * HD), jnp.float32)
        for part, pb, pc in parts:
            place = at - half * (HD // 2)
            col = place // GRP * HD + (pb * 2 + pc) * GRP + place % GRP
            pick = jnp.logical_and(at // (HD // 2) == half, to == col)
            x = x + dot(part, pick.astype(jnp.bfloat16))
        x_ref[half] = x.astype(jnp.bfloat16)
        mine = pl.ds(pl.multiple_of((b * 2 + c) * HD, HD), HD)
        out_ref[half * HD : (half + 1) * HD, :] = x_ref[half, mine, :]


def gram_kernel(r_ref, x_ref, h_ref):
    for i in range(8):
        at = i % 2 * 4 + i // 2
        part = dot(r_ref[at], x_ref[0], ATB)[0 : HD // 2] + dot(r_ref[at], x_ref[1], ATB)[HD // 2 : HD]
        for hh in range(2):
            zh, yh = (i * 2 + hh) // 4, (i * 2 + hh) % 4
            h_ref[yh * NZ + zh] = (part[hh * GRP : (hh + 1) * GRP] * (2.0 / TOKENS)).astype(jnp.bfloat16)


def call(kernel, name, outs, args, scratch=(), flops=0, moved=0, space=pltpu.VMEM, limit=40, kinds=()):
    return pl.pallas_call(
        kernel,
        out_shape=[jax.ShapeDtypeStruct(s, kind) for s, kind in zip(outs, kinds or [jnp.bfloat16] * len(outs))],
        in_specs=[pl.BlockSpec(memory_space=space)] * len(args),
        out_specs=[pl.BlockSpec(memory_space=pltpu.VMEM)] * len(outs),
        scratch_shapes=list(scratch),
        compiler_params=pltpu.CompilerParams(vmem_limit_bytes=limit << 20),
        cost_estimate=pl.CostEstimate(flops=flops, bytes_accessed=moved, transcendentals=0),
        name=name,
    )(*args)


def local(queries, keys, values):
    swap = [(0, 1), (1, 0)]
    (own,) = call(
        prep_kernel,
        "prep",
        [(NZ * NY, CUT, 2 * HD)],
        (keys, values),
        (pltpu.VMEM((2, 2, CUT, HD), jnp.bfloat16), pltpu.SemaphoreType.DMA((2, 2))),
        moved=1 << 20,
        space=pl.ANY,
        limit=60,
    )
    with jax.named_scope("q_gather"):
        near = jnp.stack([queries, lax.ppermute(queries, "xl", swap)])
        far = lax.ppermute(near, "b", swap)
    with jax.named_scope("kv_gather"):
        kv_own = lax.all_to_all(own, CHIPS, 0, 0)
        kv_own, far = lax.optimization_barrier((kv_own, far))
        kv_own = kv_own.reshape(NY, NZ, CUT, 2 * HD)
    with jax.named_scope("kv_swap"):
        kv_oth = lax.ppermute(kv_own, "c", swap)
    f32, bf16 = jnp.float32, jnp.bfloat16
    begun = call(
        begin_kernel,
        "attend_begin",
        [(2, ROWS, HD), (NZ, HD, TILE), (NZ, TILE, 2 * HD), (NZ, ROWS, TILE), (NZ, ROWS, PIECE), (2, ROWS, HD)],
        (near, far, kv_own),
        flops=1 << 31,
        limit=16,
        kinds=(bf16, bf16, bf16, f32, f32, f32),
    )
    (part,) = call(
        attend_kernel,
        "attend",
        [(NQ * 2, 2 * (HD + STAT), HD)],
        (*begun, kv_oth),
        (
            pltpu.VMEM((NZ, HD, TILE), bf16),
            pltpu.VMEM((NZ, TILE, 2 * HD), bf16),
            pltpu.VMEM((NC, NZ, ROWS, TILE), f32),
            pltpu.VMEM((ROWS, HD), f32),
            pltpu.VMEM((ROWS, 2 * HD), f32),
            pltpu.VMEM((ROWS, HD), f32),
            pltpu.VMEM((ROWS, HD), f32),
        ),
        flops=1 << 33,
        limit=28,
    )
    with jax.named_scope("part_exchange"):
        parts = lax.all_to_all(part, ("xl",) + QUAD, 0, 0)
    x0, x_many = call(combine_kernel, "combine", [(NQ * HD, HD), (8, NQ * HD, HD)], (parts,))
    with jax.named_scope("x_swap"):
        x1 = lax.ppermute(x0, "b", swap)
        x2 = lax.ppermute(jnp.stack([x0, x1]), "c", swap)
    with jax.named_scope("x_gather"):
        x_all = lax.all_to_all(x_many, ("zl", "g", "xl"), 0, 0)
    x, attn_out = call(
        assemble_kernel,
        "assemble",
        [(2, NQ * HD, 2 * HD), (TOK, 2 * HD)],
        (x0, x1, x2),
        flops=1 << 28,
        moved=1 << 20,
    )
    (gram,) = call(gram_kernel, "gram", [(NZ * NY // 2, GRP, 2 * HD)], (x_all, x))
    with jax.named_scope("h_exchange"):
        h_parts = lax.all_to_all(gram, PAIRS, 0, 0)
    hessian = jnp.sum(h_parts.astype(jnp.float32), axis=0)
    return attn_out, hessian


def solution(mesh):
    cut = Mesh(mesh.devices.reshape(NZ, NY // 2, 2, NC, 2, 2, 2), CTX + HEAD)
    in_specs = (P(CTX, HEAD), P(CTX, None), P(CTX, None))
    out_specs = (P(CTX, HEAD), P(CTX, HEAD))
    return jax.shard_map(local, mesh=cut, in_specs=in_specs, out_specs=out_specs, check_vma=False)
```
